32 devices in a mesh: dp: 8 (over z, x), tensor: 4 (over y, core).
Axes of the slice: x: 2, y: 2, z: 4, core: 2. Of those that a mesh axis runs over, the one named last changes fastest.
Arguments:
- gradient_table: bfloat16 [512, 4096], P('dp', 'tensor'), may hold values from -384 to 384
- residual_input_rows: bfloat16 [512, 4096], P('dp', 'tensor'), may hold values from -6 to 6
- act: bfloat16 [8192, 7168], P('dp', 'tensor'), may hold values from -6 to 6
- down_weight: bfloat16 [7168, 4096], P('tensor'), may hold values from -0.0625 to 0.0625
- adapter_input_factor: bfloat16 [7168, 16], P('tensor'), may hold values from -0.0625 to 0.0625
- adapter_output_factor: bfloat16 [16, 4096], replicated, may hold values from -0.75 to 0.75
- lengths: int32 [8, 64], P('dp'), may hold values from 1 to 256, 1024 in all within a row
- owning_row_index: int32 [512], replicated, may hold values from 0 to 511, as said below
Outputs:
- activation_gradient: bfloat16 [512, 7168], P('dp', 'tensor')
- adapter_input_gradient: float32 [7168, 16], P('tensor')
- adapter_output_gradient: float32 [16, 4096], P(None, 'tensor')
The draws below stay inside these ranges and needn't reach their ends.
Inputs may be any that keep to these rules, and one draw needn't show every extreme that they name: owning_row_index is a permutation of the passages; every loss owner block of 64 rows holds at most 8 passages of any one packed row, and exactly 8 for some row.
All inputs are finite; a program needn't handle non-finite values.
Results may differ from the reference program's by a relative error of at most 0.0054.
Values may be sent and summed in bfloat16 or wider, within the bound.
No kernel may reach another device: no remote copies, remote signals or barrier semaphores. Data moves between devices by JAX's collectives and lax.ppermute only.
A program may use at most 64 MiB of HBM per device.

```python
import math
import jax
import jax.numpy as jnp
import numpy as np
from jax import lax

MODEL_WIDTH = 4096
HIDDEN_IN_VIEW = 7168
ADAPTER_RANK = 16
TOK_DEV = 1024
PASS_DEV = 64
MAX_LEN = 256
PACKED = 8
PASSAGES = 512
TOKENS = 8192


def draw_owning_row_index(key, part):
    key = jax.random.fold_in(key, 7)
    first_key, second_key, third_key = jax.random.split(key, 3)
    owners = PASSAGES // PASS_DEV
    shuffled = jax.random.permutation(first_key, owners).astype(jnp.int32)
    ranking = jnp.where(shuffled == owners // 2, 0, jnp.where(shuffled == owners - 1, 1, 2)).astype(jnp.int32)
    order = jnp.argsort(ranking, stable=True)
    offsets = shuffled[order]
    within = jnp.arange(PASS_DEV, dtype=jnp.int32)
    placing = jax.random.permutation(third_key, PASS_DEV).astype(jnp.int32)
    packed_ids = jnp.arange(owners, dtype=jnp.int32)
    owner_table = (packed_ids[:, None] + offsets[placing % owners][None, :]) % owners
    slot_table = jax.vmap(lambda single: jax.random.permutation(single, PASS_DEV))(jax.random.split(second_key, owners))
    rows = owner_table * PASS_DEV + slot_table[owner_table, within[None, :]]
    return rows.reshape(-1).astype(jnp.int32)


def steps_of(rng, dims, cuts, low, high):
    def one(dim, parts):
        draws = jax.random.uniform(jax.random.fold_in(jax.random.fold_in(rng, 6), dim), (parts,), jnp.float32, low / len(cuts), high / len(cuts))
        return jnp.repeat(jnp.exp(draws), dims[dim] // parts).reshape((-1,) + (1,) * (len(dims) - dim - 1))

    factor_of = one(*cuts[0])
    for cut in cuts[1:]:
        factor_of = factor_of * one(*cut)
    return factor_of


def length_profile(amount, total, limit, skew):
    weights = [(1 << 20) // math.isqrt(rank ** skew) + 1 for rank in range(2, amount + 1)]
    surplus, counts = total - limit - (amount - 1), [1] * (amount - 1)
    while surplus > 0:
        movable = [i for i in range(amount - 1) if counts[i] < limit]
        pool, remaining = sum([weights[i] for i in movable]), surplus
        for i in movable:
            more = min(limit - counts[i], max(1, remaining * weights[i] // pool), surplus)
            counts[i] = counts[i] + more
            surplus = surplus - more
    return np.array([limit] + counts)


def ragged_sizes(own_key, number_of, total, reach, skew):
    if number_of == 2:
        one = jax.random.randint(own_key, (), max(1, total - reach), min(reach, total - 1) + 1)
        return jnp.stack([one, total - one])
    tallies = jnp.asarray(length_profile(number_of, total, reach, skew), jnp.int32)
    pairs = (number_of - 1) // 2
    source_of, sink = tallies[1:1 + 2 * pairs:2], tallies[2:2 + 2 * pairs:2]
    room = jnp.minimum(source_of - 1, reach - sink)
    moved = jax.random.randint(jax.random.fold_in(own_key, 1), (pairs,), 0, 1 << 20) % (room + 1)
    tallies = tallies.at[1:1 + 2 * pairs:2].set(source_of - moved).at[2:2 + 2 * pairs:2].set(sink + moved)
    return tallies[jax.random.permutation(jax.random.fold_in(own_key, 2), number_of)]


def gaussian(own_key, dims, scale, limit, cuts=(), held_as=jnp.bfloat16):
    entries = jax.random.normal(own_key, dims, jnp.float32) * scale
    if len(cuts) > 0:
        entries = steps_of(own_key, dims, cuts, -0.22, 0.18) * entries
    return jnp.clip(entries, min=-limit, max=limit).astype(held_as)


def setup_inputs(seed: int = 0) -> dict:
    splits = jax.random.split(jax.random.key(seed), 9)
    return {
        "gradient_table": gaussian(splits[0], (PASSAGES, MODEL_WIDTH), 64.0, 384.0, ((0, 8), (1, 4))),
        "residual_input_rows": gaussian(splits[1], (PASSAGES, MODEL_WIDTH), 1.0, 6.0, ((0, 8), (1, 4))),
        "act": gaussian(splits[2], (TOKENS, HIDDEN_IN_VIEW), 1.0, 6.0, ((0, 8), (1, 4))),
        "down_weight": gaussian(splits[3], (HIDDEN_IN_VIEW, MODEL_WIDTH), HIDDEN_IN_VIEW ** -0.5, 0.0625, ((0, 4),)),
        "adapter_input_factor": gaussian(splits[4], (HIDDEN_IN_VIEW, ADAPTER_RANK), HIDDEN_IN_VIEW ** -0.5, 0.0625, ((0, 4),)),
        "adapter_output_factor": gaussian(splits[5], (ADAPTER_RANK, MODEL_WIDTH), (4 * ADAPTER_RANK) ** -0.5, 0.75),
        "lengths": jax.vmap(lambda own: ragged_sizes(own, PASS_DEV, TOK_DEV, MAX_LEN, 2))(jax.random.split(splits[6], PACKED)).reshape((PACKED, PASS_DEV)).astype(jnp.int32),
        "owning_row_index": draw_owning_row_index(jax.random.fold_in(splits[8], 71), 0),
    }


ADAPTER_SCALE = 2.0
EPSILON = 1e-06

def reference(gradient_table, residual_input_rows, act, down_weight, adapter_input_factor, adapter_output_factor, lengths, owning_row_index):
    endings = jnp.cumsum(lengths, axis=1) - 1
    offsets = (jnp.arange(lengths.shape[0], dtype=jnp.int32) * TOK_DEV)[:, None]
    positions = (endings + offsets).reshape(-1).astype(jnp.int32)
    pooled_embedding = act[positions]
    partial_result_value = jnp.dot(pooled_embedding, down_weight, preferred_element_type=jnp.float32)
    reduced_output_factor = jnp.dot(pooled_embedding, adapter_input_factor, preferred_element_type=jnp.float32).astype(jnp.bfloat16)
    hidden_output = partial_result_value + residual_input_rows.astype(jnp.float32) + ADAPTER_SCALE * jnp.dot(reduced_output_factor, adapter_output_factor, preferred_element_type=jnp.float32)
    grads = gradient_table[owning_row_index].astype(jnp.float32)
    length = jnp.sqrt(lax.optimization_barrier(jnp.sum(hidden_output * hidden_output, axis=1, keepdims=True)) + EPSILON)
    unit = hidden_output / length
    along = lax.optimization_barrier(jnp.sum(grads * unit, axis=1, keepdims=True))
    unit_direction = ((grads - along * unit) / length).astype(jnp.bfloat16)
    broadcast_gradient = jnp.dot(unit_direction, adapter_output_factor.T, preferred_element_type=jnp.float32).astype(jnp.bfloat16)
    activation_gradient = (jnp.dot(unit_direction, down_weight.T, preferred_element_type=jnp.float32) + ADAPTER_SCALE * jnp.dot(broadcast_gradient, adapter_input_factor.T, preferred_element_type=jnp.float32)).astype(jnp.bfloat16)
    passage_count = positions.shape[0]
    adapter_input_gradient = ADAPTER_SCALE * jnp.dot(pooled_embedding.T, broadcast_gradient, preferred_element_type=jnp.float32) / passage_count
    adapter_output_gradient = ADAPTER_SCALE * jnp.dot(reduced_output_factor.T, unit_direction, preferred_element_type=jnp.float32) / passage_count
    return (activation_gradient, adapter_input_gradient, adapter_output_gradient)
```

```python
import functools

import jax
import jax.numpy as jnp
from jax import lax
from jax.experimental import pallas as pl
from jax.experimental.pallas import tpu as pltpu
from jax.sharding import PartitionSpec as P

ADAPTER_SCALE = 2.0
EPSILON = 1e-06
F32, BF16 = jnp.float32, jnp.bfloat16
LANES = 128
ROWS = 256
VMEM = pl.BlockSpec(memory_space=pltpu.VMEM)
SMEM = pl.BlockSpec(memory_space=pltpu.SMEM)


def dot(a, b, dims=((1,), (0,))):
    return lax.dot_general(a, b, (dims, ((), ())), preferred_element_type=F32)


def call(body, outs, name, *args, near=(), far=(), after=(), scratch=(), flops=0, limit=24):
    size = sum(a.size * a.dtype.itemsize for a in args + near + far)
    specs = [SMEM if a.dtype == jnp.int32 and a.size == 1 else VMEM for a in args]
    specs += [pl.BlockSpec(memory_space=pltpu.HBM)] * (len(near) + len(far) + len(after))
    held = [pltpu.VMEM(a.shape, a.dtype) for a in near]
    held += [pltpu.SemaphoreType.DMA((len(near),))] if near else []

    def run(*refs):
        refs = list(refs)
        inputs = [refs.pop(0) for _ in args]
        distant = [refs.pop(0) for _ in near]
        inputs += [refs.pop(0) for _ in far]
        del refs[: len(after)]
        if near:
            sems = refs.pop()
            here = refs[len(refs) - len(near) :]
            del refs[len(refs) - len(near) :]
            copies = [pltpu.make_async_copy(a, b, sems.at[i]) for i, (a, b) in enumerate(zip(distant, here))]
            for copy in copies:
                copy.start()
            inputs = (inputs, here, copies)
            body(inputs, *refs)
        else:
            body(*inputs, *refs)

    return pl.pallas_call(
        run,
        out_shape=[jax.ShapeDtypeStruct(*s) for s in outs],
        in_specs=specs,
        out_specs=[VMEM] * len(outs),
        scratch_shapes=list(scratch) + held,
        compiler_params=pltpu.CompilerParams(vmem_limit_bytes=limit << 20),
        cost_estimate=pl.CostEstimate(flops=flops, bytes_accessed=size, transcendentals=0),
        name=name,
    )(*args, *[pltpu.with_memory_space_constraint(a, pltpu.HBM) for a in near + far + after])


def cuts(total, step):
    return [(at, min(step, total - at)) for at in range(0, total, step)]


def iota(shape, dim):
    return lax.broadcasted_iota(jnp.int32, shape, dim)


def turned(column):
    n = column.shape[0]
    return jnp.sum(jnp.where(iota((n, n), 0) == iota((n, n), 1), column, 0), axis=0, keepdims=True)


def route_body(passes, capacity, inputs, out_ref):
    (device_ref,), (index_ref, table_ref), copies = inputs
    rows, slots = table_ref.shape[0], out_ref.shape[0]
    copies[0].wait()
    index = index_ref[...]
    total = index.shape[1]
    mine = device_ref[0] * rows + iota((rows, total), 0)
    packed = iota((rows, total), 1) // passes
    dest = jnp.sum(jnp.where(index == mine, packed, 0), axis=1, keepdims=True)
    earlier = (dest == turned(dest)) & (iota((rows, rows), 1) < iota((rows, rows), 0))
    rank = jnp.sum(earlier.astype(jnp.int32), axis=1, keepdims=True)
    slot = turned(dest * capacity + rank)
    picker = (iota((slots, rows), 0) == slot).astype(F32).astype(BF16)
    copies[1].wait()
    out_ref[...] = dot(picker, table_ref[...]).astype(BF16)


def slot_picker(index_ref, owners, owned, capacity):
    row = index_ref[...]
    n = row.shape[1]
    column = jnp.sum(jnp.where(iota((n, n), 0) == iota((n, n), 1), row, 0), axis=1, keepdims=True)
    owner = column // owned
    earlier = (owner == row // owned) & (row < column)
    slot = owner * capacity + jnp.sum(earlier.astype(jnp.int32), axis=1, keepdims=True)
    return (slot == iota((n, owners * capacity), 1)).astype(F32).astype(BF16)


def start_all(source_ref, held_ref, sems, dim, step, offset=0, size=None):
    copies = []
    for i, (at, n) in enumerate(cuts(held_ref.shape[dim], step)):
        piece = slice(at, at + n)
        to = held_ref.at[piece] if dim == 0 else held_ref.at[:, piece]
        if dim == 1:
            source = source_ref.at[:, piece]
        else:
            source = source_ref.at[piece, pl.ds(pl.multiple_of(offset, LANES), size)]
        copies.append(pltpu.make_async_copy(source, to, sems.at[i]))
    return copies


def own_terms(half, member, residual_ref, out_ref):
    columns = residual_ref.shape[1]
    blocks = out_ref.shape[1] // columns
    for j in range(blocks):
        own = jnp.where(half * blocks + j == member, 1.0, 0.0)
        out_ref[:, j * columns : (j + 1) * columns] = own * residual_ref[...].astype(F32)
    out_ref[:, blocks * columns :] = jnp.zeros_like(out_ref[:, blocks * columns :])


def add_low(half, low, factor_ref, out_ref, width):
    columns = pl.ds(pl.multiple_of(half * width, LANES), width)
    out_ref[:, :width] += ADAPTER_SCALE * dot(low.astype(BF16), factor_ref[:, columns])
    out_ref[:, width : width + low.shape[1]] = low


def first_body(inputs, out_ref, pooled_ref, low_ref, act_held, weight_held, act_sems, sems):
    (member_ref, act_ref, weight_ref), (lengths_ref, residual_ref, input_factor_ref, factor_ref), copies = inputs
    member = member_ref[0]
    half = 1 - member % 2
    hidden, width = weight_held.shape
    acts = start_all(act_ref, act_held, act_sems, 1, ROWS)
    weights = start_all(weight_ref, weight_held, sems, 0, ROWS, half * width, width)
    for pair in zip(acts, weights):
        for copy in pair:
            copy.start()
    for copy in copies:
        copy.wait()
    lengths = lengths_ref[...]
    n = lengths.shape[1]
    upto = jnp.where(iota((n, n), 1) <= iota((n, n), 0), lengths, 0)
    last = jnp.sum(upto, axis=1, keepdims=True) - 1
    picker = (last == iota((n, act_ref.shape[0]), 1)).astype(F32).astype(BF16)
    own_terms(half, member, residual_ref, out_ref)
    low = jnp.zeros(low_ref.shape, F32)
    for (at, size), act_copy, weight_copy in zip(cuts(hidden, ROWS), acts, weights):
        piece = slice(at, at + size)
        act_copy.wait()
        pooled = dot(picker, act_held[:, piece]).astype(BF16)
        pooled_ref[:, piece] = pooled
        low += dot(pooled, input_factor_ref[:, piece], ((1,), (1,)))
        weight_copy.wait()
        out_ref[:, :width] += dot(pooled, weight_held[piece, :])
    low_ref[...] = low
    add_low(half, low, factor_ref, out_ref, width)


def second_body(inputs, out_ref, weight_held, sems):
    (member_ref, pooled_ref, low_ref, weight_ref), (residual_ref, factor_ref), copies = inputs
    member = member_ref[0]
    half = member % 2
    hidden, width = weight_held.shape
    weights = start_all(weight_ref, weight_held, sems, 0, ROWS, half * width, width)
    for copy in weights:
        copy.start()
    for copy in copies:
        copy.wait()
    own_terms(half, member, residual_ref, out_ref)
    add_low(half, low_ref[...], factor_ref, out_ref, width)
    for (at, size), copy in zip(cuts(hidden, ROWS), weights):
        piece = slice(at, at + size)
        copy.wait()
        out_ref[:, :width] += dot(pooled_ref[:, piece], weight_held[piece, :])


def sum_body(width, rank, *refs):
    *ins, sum_ref, out_ref = refs
    total = ins[0][...] + ins[1][...]
    sum_ref[...] = total
    out_ref[:, :width] = total[:, :width].astype(BF16)
    low = total[:, width : width + rank]
    high = low.astype(BF16)
    out_ref[:, width:] = jnp.zeros_like(out_ref[:, width:])
    out_ref[:, width : width + rank] = high
    out_ref[:, width + rank : width + 2 * rank] = (low - high.astype(F32)).astype(BF16)


def add_body(width, rank, sum_ref, got_ref, total_ref, out_ref):
    total = sum_ref[:, :width] + got_ref[:, :width].astype(F32)
    total_ref[:, :width] = total
    out_ref[:, :width] = total.astype(BF16)
    low = (
        sum_ref[:, width : width + rank]
        + got_ref[:, width : width + rank].astype(F32)
        + got_ref[:, width + rank : width + 2 * rank].astype(F32)
    )
    total_ref[:, width:] = jnp.zeros_like(total_ref[:, width:])
    total_ref[:, width : width + rank] = low
    high = low.astype(BF16)
    out_ref[:, width:] = jnp.zeros_like(out_ref[:, width:])
    out_ref[:, width : width + rank] = high
    out_ref[:, width + rank : width + 2 * rank] = (low - high.astype(F32)).astype(BF16)


def direction_body(owners, owned, capacity, count, member_ref, index_ref, mine_ref, other_ref, grads_ref, factor_ref,
                   pooled_ref, direction_ref, spread_ref, packed_ref):
    member = member_ref[0]
    core = member % 2
    width = other_ref.shape[1]
    rank, model = factor_ref.shape
    mine = mine_ref[:, :width]
    other = other_ref[...].astype(F32)
    low = mine_ref[:, width : width + rank].astype(BF16)
    squares = jnp.sum(mine * mine, axis=1, keepdims=True) + jnp.sum(other * other, axis=1, keepdims=True)
    length = jnp.sqrt(squares + EPSILON)
    picker = slot_picker(index_ref, owners, owned, capacity)
    first = jnp.where(core == 0, mine, other)
    second = jnp.where(core == 0, other, mine)
    unit = [first / length, second / length]
    grads = [dot(picker, grads_ref[:, i * width : (i + 1) * width]) for i in range(2)]
    along = sum(jnp.sum(g * u, axis=1, keepdims=True) for g, u in zip(grads, unit))
    for i in range(2):
        direction_ref[:, i * width : (i + 1) * width] = ((grads[i] - along * unit[i]) / length).astype(BF16)
    spread = dot(direction_ref[...], factor_ref[...], ((1,), (1,))).astype(BF16)
    spread_ref[...] = spread
    hidden = pooled_ref.shape[1]
    columns = packed_ref.shape[1] - hidden
    scale = ADAPTER_SCALE / count
    packed_ref[:, :hidden] = (scale * dot(spread, pooled_ref[...], ((0,), (0,)))).astype(BF16)
    own = direction_ref[:, pl.ds(pl.multiple_of(member * columns, LANES), columns)]
    packed_ref[:, hidden:] = (scale * dot(low, own, ((0,), (0,)))).astype(BF16)


def round_sum_body(own_ref, got_ref, *refs):
    refs[-1][...] = (own_ref[...].astype(F32) + got_ref[...].astype(F32)).astype(BF16)


def last_sum_body(own_ref, got_ref, *refs):
    first_ref, second_ref = refs[-2:]
    total = own_ref[...].astype(F32) + got_ref[...].astype(F32)
    hidden = first_ref.shape[1]
    first_ref[...] = total[:, :hidden]
    second_ref[...] = total[:, hidden:]


def activation_body(start, stop, *refs):
    direction_ref, spread_ref, input_factor_ref = refs[:3]
    weight_ref, out_ref, token_ref, held, sems = refs[-5:]
    token_ref[...] = jnp.zeros_like(token_ref)
    whole = (stop - start) // ROWS

    def load(i, at, size):
        to = held.at[i] if size == ROWS else held.at[i, :size]
        return pltpu.make_async_copy(weight_ref.at[pl.ds(at, size)], to, sems.at[i])

    def part(i, at, size):
        columns = pl.ds(at, size)
        value = ADAPTER_SCALE * dot(spread_ref[...], input_factor_ref[:, columns])
        load(i, at, size).wait()
        rows = held[i] if size == ROWS else held[i, :size]
        out_ref[:, columns] = (value + dot(direction_ref[...], rows, ((1,), (1,)))).astype(BF16)

    for i, (at, size) in enumerate(cuts(stop - start, ROWS)):
        load(i, start + at, size).start()
    if start:
        out_ref[:, :start] = refs[3][:, :start]

    @pl.loop(0, whole)
    def _(i):
        part(i, pl.multiple_of(start + i * ROWS, ROWS), ROWS)

    if whole * ROWS < stop - start:
        part(whole, start + whole * ROWS, stop - start - whole * ROWS)


def local(gradient_table, residual_input_rows, act, down_weight, adapter_input_factor, adapter_output_factor, lengths,
          owning_row_index):
    devices = lax.axis_size("dp")
    members = lax.axis_size("tensor")
    device = lax.axis_index("dp")
    member = lax.axis_index("tensor")
    passes = lengths.shape[1]
    owned, columns = gradient_table.shape
    rank, model = adapter_output_factor.shape
    hidden = act.shape[1]
    capacity = -(-passes // devices)
    slots = devices * capacity
    blocks = members // 2
    width = blocks * columns
    count = passes * devices
    dp_at = device.astype(jnp.int32).reshape(1)
    member_at = member.astype(jnp.int32).reshape(1)
    input_factor = adapter_input_factor.T

    def swap(x, axis, size, bit):
        return lax.ppermute(x, axis, [(i, i ^ bit) for i in range(size)])

    steps = []
    bit = 2
    while bit < members:
        steps.append(bit)
        bit *= 2

    index = owning_row_index.reshape(1, -1)
    (sent,) = call(functools.partial(route_body, passes, capacity), [((slots, columns), BF16)], "route",
                   dp_at, near=(index, gradient_table))
    routed = lax.all_to_all(sent, "dp", 0, 0, tiled=True)
    grads = routed
    parts = {0: routed}
    for bit in steps:
        parts.update({k ^ bit: swap(v, "tensor", members, bit) for k, v in list(parts.items())})
    parts.update({k ^ 1: swap(v, "tensor", members, 1) for k, v in list(parts.items())})

    half_shape = (passes, width + LANES)
    pieces = len(cuts(hidden, ROWS))
    holds = [pltpu.VMEM((hidden, width), BF16)]
    sems = [pltpu.SemaphoreType.DMA((pieces,))]
    out, pooled, low = call(
        first_body, [(half_shape, F32), ((passes, hidden), BF16), ((passes, rank), F32)], "project_away",
        member_at, near=(lengths, residual_input_rows, input_factor, adapter_output_factor), far=(act, down_weight),
        scratch=[pltpu.VMEM(act.shape, BF16), *holds, *sems, *sems],
        flops=passes * hidden * model, after=(sent,),
    )
    away = swap(out, "tensor", members, 1)
    (kept,) = call(
        second_body, [(half_shape, F32)], "project_own",
        member_at, pooled, low, near=(residual_input_rows, adapter_output_factor), far=(down_weight,),
        scratch=[*holds, *sems], flops=passes * hidden * model,
    )
    total, out = call(functools.partial(sum_body, width, rank), [(half_shape, F32), (half_shape, BF16)], "sum_cores",
                      kept, away)
    for bit in steps:
        got = swap(out, "tensor", members, bit)
        total, out = call(functools.partial(add_body, width, rank), [(half_shape, F32), (half_shape, BF16)],
                          "sum_chips", total, got)
    other = swap(out[:, :width], "tensor", members, 1)

    ordered = jnp.stack([parts[k] for k in range(members)])
    grads = jnp.concatenate(
        [lax.dynamic_index_in_dim(ordered, member ^ b, 0, keepdims=False) for b in range(members)], axis=1
    )
    my_index = lax.dynamic_slice_in_dim(owning_row_index, device * passes, passes).reshape(1, -1)
    direction, spread, packed = call(
        functools.partial(direction_body, devices, owned, capacity, count),
        [((passes, model), BF16), ((passes, rank), BF16), ((rank, hidden + columns), BF16)], "direction",
        member_at, my_index, total, other, grads, adapter_output_factor, pooled,
        flops=passes * model * 64,
    )
    parts = 3
    ends = [min(hidden, -(-pieces * (i + 1) // parts) * ROWS) for i in range(parts)]
    token = []
    activation = []

    def activate():
        start = ends[len(ends) - len(todo) - 1] if len(todo) < parts else 0
        stop = todo.pop(0)
        out, done = call(
            functools.partial(activation_body, start, stop), [((passes, hidden), BF16), ((8, LANES), F32)], "activation",
            direction, spread, input_factor, *activation, far=(down_weight,),
            scratch=[
                pltpu.VMEM((-(-(stop - start) // ROWS), ROWS, model), BF16),
                pltpu.SemaphoreType.DMA((-(-(stop - start) // ROWS),)),
            ],
            flops=passes * (stop - start) * model * 2,
        )
        activation[:] = [out]
        token[:] = [done]

    todo = list(ends)
    shapes = [((rank, hidden), F32), ((rank, columns), F32)]
    if devices & (devices - 1) == 0:
        bit = 1
        while bit < devices:
            got = swap(packed, "dp", devices, bit)
            bit *= 2
            if todo:
                activate()
            if bit < devices:
                (packed,) = call(round_sum_body, [(packed.shape, BF16)], "sum_pairs", packed, got, *token)
            else:
                sums = call(last_sum_body, shapes, "sum_last", packed, got, *token)
    else:
        packed = lax.psum(packed.astype(F32), "dp")
        sums = packed[:, :hidden], packed[:, hidden:]
    while todo:
        activate()
    return activation[0], sums[0].T, sums[1]


def solution(mesh):
    placed = (
        P("dp", "tensor"),
        P("dp", "tensor"),
        P("dp", "tensor"),
        P("tensor", None),
        P("tensor", None),
        P(),
        P("dp", None),
        P(),
    )
    return jax.shard_map(
        local,
        mesh=mesh,
        in_specs=placed,
        out_specs=(P("dp", "tensor"), P("tensor", None), P(None, "tensor")),
        check_vma=False,
    )
```

```python
import functools

import jax
import jax.numpy as jnp
from jax import lax
from jax.experimental import pallas as pl
from jax.experimental.pallas import tpu as pltpu
from jax.sharding import PartitionSpec as P

ADAPTER_SCALE = 2.0
EPSILON = 1e-06
F32, BF16 = jnp.float32, jnp.bfloat16
LANES = 128
ROWS = 256
VMEM = pl.BlockSpec(memory_space=pltpu.VMEM)
SMEM = pl.BlockSpec(memory_space=pltpu.SMEM)


def dot(a, b, dims=((1,), (0,))):
    return lax.dot_general(a, b, (dims, ((), ())), preferred_element_type=F32)


def call(body, outs, name, *args, near=(), far=(), after=(), scratch=(), flops=0, limit=24):
    size = sum(a.size * a.dtype.itemsize for a in args + near + far)
    specs = [SMEM if a.dtype == jnp.int32 and a.size == 1 else VMEM for a in args]
    specs += [pl.BlockSpec(memory_space=pltpu.HBM)] * (len(near) + len(far) + len(after))
    held = [pltpu.VMEM(a.shape, a.dtype) for a in near]
    held += [pltpu.SemaphoreType.DMA((len(near),))] if near else []

    def run(*refs):
        refs = list(refs)
        inputs = [refs.pop(0) for _ in args]
        distant = [refs.pop(0) for _ in near]
        inputs += [refs.pop(0) for _ in far]
        del refs[: len(after)]
        if near:
            sems = refs.pop()
            here = refs[len(refs) - len(near) :]
            del refs[len(refs) - len(near) :]
            copies = [pltpu.make_async_copy(a, b, sems.at[i]) for i, (a, b) in enumerate(zip(distant, here))]
            for copy in copies:
                copy.start()
            inputs = (inputs, here, copies)
            body(inputs, *refs)
        else:
            body(*inputs, *refs)

    return pl.pallas_call(
        run,
        out_shape=[jax.ShapeDtypeStruct(*s) if isinstance(s, tuple) else s for s in outs],
        in_specs=specs,
        out_specs=[VMEM if isinstance(s, tuple) else pl.BlockSpec(memory_space=pltpu.HBM) for s in outs],
        scratch_shapes=list(scratch) + held,
        compiler_params=pltpu.CompilerParams(vmem_limit_bytes=limit << 20),
        cost_estimate=pl.CostEstimate(flops=flops, bytes_accessed=size, transcendentals=0),
        name=name,
    )(*args, *[pltpu.with_memory_space_constraint(a, pltpu.HBM) for a in near + far + after])


def cuts(total, step):
    return [(at, min(step, total - at)) for at in range(0, total, step)]


def iota(shape, dim):
    return lax.broadcasted_iota(jnp.int32, shape, dim)


def turned(column):
    n = column.shape[0]
    return jnp.sum(jnp.where(iota((n, n), 0) == iota((n, n), 1), column, 0), axis=0, keepdims=True)


def route_body(passes, capacity, inputs, out_ref):
    (device_ref,), (index_ref, table_ref), copies = inputs
    rows, slots = table_ref.shape[0], out_ref.shape[0]
    copies[0].wait()
    index = index_ref[...]
    total = index.shape[1]
    mine = device_ref[0] * rows + iota((rows, total), 0)
    packed = iota((rows, total), 1) // passes
    dest = jnp.sum(jnp.where(index == mine, packed, 0), axis=1, keepdims=True)
    earlier = (dest == turned(dest)) & (iota((rows, rows), 1) < iota((rows, rows), 0))
    rank = jnp.sum(earlier.astype(jnp.int32), axis=1, keepdims=True)
    slot = turned(dest * capacity + rank)
    picker = (iota((slots, rows), 0) == slot).astype(F32).astype(BF16)
    copies[1].wait()
    out_ref[...] = dot(picker, table_ref[...]).astype(BF16)


def slot_picker(index_ref, owners, owned, capacity):
    row = index_ref[...]
    n = row.shape[1]
    column = jnp.sum(jnp.where(iota((n, n), 0) == iota((n, n), 1), row, 0), axis=1, keepdims=True)
    owner = column // owned
    earlier = (owner == row // owned) & (row < column)
    slot = owner * capacity + jnp.sum(earlier.astype(jnp.int32), axis=1, keepdims=True)
    return (slot == iota((n, owners * capacity), 1)).astype(F32).astype(BF16)


def project_body(inputs, out_ref, pooled_ref, low_ref, act_held, weight_held, act_sems, sems):
    (member_ref, lengths_ref, act_ref, weight_ref), (residual_ref, input_factor_ref), copies = inputs
    hidden = weight_held.shape[0]
    pieces = []
    for i, (at, size) in enumerate(cuts(hidden, ROWS)):
        piece = slice(at, at + size)
        act_copy = pltpu.make_async_copy(act_ref.at[:, piece], act_held.at[:, piece], act_sems.at[i])
        act_copy.start()
        copy = pltpu.make_async_copy(weight_ref.at[piece], weight_held.at[piece], sems.at[i])
        copy.start()
        pieces.append((piece, act_copy, copy))
    lengths = lengths_ref[...]
    n = lengths.shape[1]
    upto = jnp.where(iota((n, n), 1) <= iota((n, n), 0), lengths, 0)
    last = jnp.sum(upto, axis=1, keepdims=True) - 1
    picker = (last == iota((n, act_ref.shape[0]), 1)).astype(F32).astype(BF16)
    for piece, act_copy, copy in pieces:
        act_copy.wait()
        pooled = dot(picker, act_held[:, piece]).astype(BF16)
        pooled_ref[:, piece] = pooled
        copy.wait()
        value = dot(pooled, weight_held[piece, :])
        if piece.start == 0:
            out_ref[...] = value
        else:
            out_ref[...] += value
    for copy in copies:
        copy.wait()
    low_ref[...] = dot(pooled_ref[...], input_factor_ref[...], ((1,), (1,)))
    columns = residual_ref.shape[1]
    own = pl.ds(pl.multiple_of(member_ref[0] * columns, LANES), columns)
    out_ref[:, own] += residual_ref[...].astype(F32)


def half_of(half, width, parts_ref, low_ref, factor_ref):
    columns = pl.ds(pl.multiple_of(half * width, LANES), width)
    return parts_ref[:, columns] + ADAPTER_SCALE * dot(low_ref[...].astype(BF16), factor_ref[:, columns])


def finish_body(owners, owned, capacity, member_ref, index_ref, routed_ref, parts_ref, low_ref, factor_ref, away_ref,
                grads_ref):
    width, rank = parts_ref.shape[1] // 2, low_ref.shape[1]
    away_ref[:, :width] = half_of(1 - member_ref[0] % 2, width, parts_ref, low_ref, factor_ref)
    away_ref[:, width:] = jnp.zeros_like(away_ref[:, width:])
    away_ref[:, width : width + rank] = low_ref[...]
    grads_ref[...] = dot(slot_picker(index_ref, owners, owned, capacity), routed_ref[...]).astype(BF16)


def put_low(low, at, out_ref):
    rank = low.shape[1]
    high = low.astype(BF16)
    out_ref[:, at:] = jnp.zeros_like(out_ref[:, at:])
    out_ref[:, at : at + rank] = high
    out_ref[:, at + rank : at + 2 * rank] = (low - high.astype(F32)).astype(BF16)


def sum_cores_body(member_ref, parts_ref, low_ref, away_ref, factor_ref, total_ref, low_total_ref, out_ref):
    width, rank = parts_ref.shape[1] // 2, low_ref.shape[1]
    total = half_of(member_ref[0] % 2, width, parts_ref, low_ref, factor_ref) + away_ref[:, :width]
    low = low_ref[...] + away_ref[:, width : width + rank]
    total_ref[...] = total
    low_total_ref[...] = low
    out_ref[:, :width] = total.astype(BF16)
    put_low(low, width, out_ref)


def sum_chips_body(last, total_ref, low_ref, got_ref, grads_ref, got_grads_ref, new_total_ref, new_low_ref, out_ref,
                   *more):
    width, rank = total_ref.shape[1], low_ref.shape[1]
    total = total_ref[...] + got_ref[:, :width].astype(F32)
    low = low_ref[...]
    for i in range(2):
        low += got_ref[:, width + i * rank : width + (i + 1) * rank].astype(F32)
    new_total_ref[...] = total
    new_low_ref[...] = low
    out_ref[:, :width] = total.astype(BF16)
    columns = grads_ref.shape[1]
    if last:
        joined_ref, at = out_ref, width
    else:
        put_low(low, width, out_ref)
        (joined_ref,), at = more, 0
    joined_ref[:, at : at + columns] = grads_ref[...]
    joined_ref[:, at + columns : at + 2 * columns] = got_grads_ref[...]


def direction_body(count, blocks, member_ref, total_ref, low_ref, mine_ref, other_ref, factor_ref, pooled_ref,
                   direction_ref, spread_ref, packed_ref):
    member = member_ref[0]
    width = total_ref.shape[1]
    columns = width // blocks

    def hidden_block(b):
        piece = slice(b % blocks * columns, (b % blocks + 1) * columns)
        return jnp.where(member % 2 == b // blocks, total_ref[:, piece], other_ref[:, piece].astype(F32))

    def grads_block(b):
        apart = member ^ b
        piece = pl.ds(pl.multiple_of(width + apart // 2 * columns, LANES), columns)
        return jnp.where(apart % 2 == 0, mine_ref[:, piece].astype(F32), other_ref[:, piece].astype(F32))

    squares = sum(jnp.sum(hidden_block(b) ** 2, axis=1, keepdims=True) for b in range(2 * blocks))
    length = jnp.sqrt(squares + EPSILON)
    along = sum(
        jnp.sum(grads_block(b) * (hidden_block(b) / length), axis=1, keepdims=True) for b in range(2 * blocks)
    )
    for b in range(2 * blocks):
        value = (grads_block(b) - along * (hidden_block(b) / length)) / length
        direction_ref[:, b * columns : (b + 1) * columns] = value.astype(BF16)
    spread = dot(direction_ref[...], factor_ref[...], ((1,), (1,))).astype(BF16)
    spread_ref[...] = spread
    hidden = pooled_ref.shape[1]
    scale = ADAPTER_SCALE / count
    packed_ref[:, :hidden] = (scale * dot(spread, pooled_ref[...], ((0,), (0,)))).astype(BF16)
    own = direction_ref[:, pl.ds(pl.multiple_of(member * columns, LANES), columns)]
    packed_ref[:, hidden:] = (scale * dot(low_ref[...].astype(BF16), own, ((0,), (0,)))).astype(BF16)


def round_sum_body(own_ref, got_ref, *refs):
    refs[-1][...] = (own_ref[...].astype(F32) + got_ref[...].astype(F32)).astype(BF16)


def last_sum_body(own_ref, got_ref, *refs):
    first_ref, second_ref = refs[-2:]
    total = own_ref[...].astype(F32) + got_ref[...].astype(F32)
    hidden = first_ref.shape[1]
    first_ref[...] = total[:, :hidden]
    second_ref[...] = total[:, hidden:]


def activation_body(start, stop, *refs):
    direction_ref, spread_ref, input_factor_ref = refs[:3]
    weight_ref, out_ref, token_ref, held, sems = refs[-5:]
    token_ref[...] = jnp.zeros_like(token_ref)
    whole = (stop - start) // ROWS

    def load(i, at, size):
        to = held.at[i] if size == ROWS else held.at[i, :size]
        return pltpu.make_async_copy(weight_ref.at[pl.ds(at, size)], to, sems.at[i])

    def part(i, at, size):
        columns = pl.ds(at, size)
        value = ADAPTER_SCALE * dot(spread_ref[...], input_factor_ref[:, columns])
        load(i, at, size).wait()
        rows = held[i] if size == ROWS else held[i, :size]
        out_ref[:, columns] = (value + dot(direction_ref[...], rows, ((1,), (1,)))).astype(BF16)

    for i, (at, size) in enumerate(cuts(stop - start, ROWS)):
        load(i, start + at, size).start()
    if start:
        out_ref[:, :start] = refs[3][:, :start]

    @pl.loop(0, whole)
    def _(i):
        part(i, pl.multiple_of(start + i * ROWS, ROWS), ROWS)

    if whole * ROWS < stop - start:
        part(whole, start + whole * ROWS, stop - start - whole * ROWS)


def local(gradient_table, residual_input_rows, act, down_weight, adapter_input_factor, adapter_output_factor, lengths,
          owning_row_index):
    devices = lax.axis_size("dp")
    members = lax.axis_size("tensor")
    device = lax.axis_index("dp")
    member = lax.axis_index("tensor")
    passes = lengths.shape[1]
    owned, columns = gradient_table.shape
    rank, model = adapter_output_factor.shape
    hidden = act.shape[1]
    capacity = -(-passes // devices)
    slots = devices * capacity
    blocks = members // 2
    width = blocks * columns
    count = passes * devices
    dp_at = device.astype(jnp.int32).reshape(1)
    member_at = member.astype(jnp.int32).reshape(1)
    input_factor = adapter_input_factor.T

    def swap(x, axis, size, bit):
        return lax.ppermute(x, axis, [(i, i ^ bit) for i in range(size)])

    steps = []
    bit = 2
    while bit < members:
        steps.append(bit)
        bit *= 2

    index = owning_row_index.reshape(1, -1)
    my_index = lax.dynamic_slice_in_dim(owning_row_index, device * passes, passes).reshape(1, -1)
    (sent,) = call(
        functools.partial(route_body, passes, capacity), [((slots, columns), BF16)], "route",
        dp_at, near=(index, gradient_table),
    )
    routed = lax.all_to_all(sent, "dp", 0, 0, tiled=True)
    pieces = len(cuts(hidden, ROWS))
    terms, pooled, low = call(
        project_body, [((passes, model), F32), ((passes, hidden), BF16), ((passes, rank), F32)], "project",
        member_at, lengths, near=(residual_input_rows, input_factor), far=(act, down_weight),
        scratch=[pltpu.VMEM(act.shape, BF16), pltpu.VMEM(down_weight.shape, BF16)]
        + [pltpu.SemaphoreType.DMA((pieces,))] * 2,
        flops=2 * passes * hidden * model, limit=32,
    )
    away, grads = call(
        functools.partial(finish_body, devices, owned, capacity),
        [((passes, width + LANES), F32), ((passes, columns), BF16)], "finish",
        member_at, my_index, routed, terms, low, adapter_output_factor,
    )
    away = swap(away, "tensor", members, 1)
    sums = [((passes, width), F32), ((passes, rank), F32)]
    total, low, out = call(
        sum_cores_body, [*sums, ((passes, width + LANES), BF16)], "sum_cores",
        member_at, terms, low, away, adapter_output_factor,
    )
    for bit in steps:
        got, got_grads = swap(out, "tensor", members, bit), swap(grads, "tensor", members, bit)
        joined = 2 * grads.shape[1]
        last = bit == steps[-1]
        outs = [((passes, width + joined), BF16)] if last else [(out.shape, BF16), ((passes, joined), BF16)]
        total, low, out, *more = call(
            functools.partial(sum_chips_body, last), [*sums, *outs], "sum_chips",
            total, low, got, grads, got_grads,
        )
        grads = more[0] if more else None
    other = swap(out, "tensor", members, 1)
    direction, spread, packed = call(
        functools.partial(direction_body, count, blocks),
        [((passes, model), BF16), ((passes, rank), BF16), ((rank, hidden + columns), BF16)], "direction",
        member_at, total, low, out, other, adapter_output_factor, pooled,
        flops=passes * model * 64,
    )
    parts = 3
    ends = [min(hidden, -(-pieces * (i + 1) // parts) * ROWS) for i in range(parts)]
    token = []
    activation = []

    def activate():
        start = ends[len(ends) - len(todo) - 1] if len(todo) < parts else 0
        stop = todo.pop(0)
        out, done = call(
            functools.partial(activation_body, start, stop), [((passes, hidden), BF16), ((8, LANES), F32)], "activation",
            direction, spread, input_factor, *activation, far=(down_weight,),
            scratch=[
                pltpu.VMEM((-(-(stop - start) // ROWS), ROWS, model), BF16),
                pltpu.SemaphoreType.DMA((-(-(stop - start) // ROWS),)),
            ],
            flops=passes * (stop - start) * model * 2,
        )
        activation[:] = [out]
        token[:] = [done]

    todo = list(ends)
    shapes = [((rank, hidden), F32), ((rank, columns), F32)]
    if devices & (devices - 1) == 0:
        bit = 1
        while bit < devices:
            got = swap(packed, "dp", devices, bit)
            bit *= 2
            if todo:
                activate()
            if bit < devices:
                (packed,) = call(round_sum_body, [(packed.shape, BF16)], "sum_pairs", packed, got, *token)
            else:
                sums = call(last_sum_body, shapes, "sum_last", packed, got, *token)
    else:
        packed = lax.psum(packed.astype(F32), "dp")
        sums = packed[:, :hidden], packed[:, hidden:]
    while todo:
        activate()
    return activation[0], sums[0].T, sums[1]


def solution(mesh):
    placed = (
        P("dp", "tensor"),
        P("dp", "tensor"),
        P("dp", "tensor"),
        P("tensor", None),
        P("tensor", None),
        P(),
        P("dp", None),
        P(),
    )
    return jax.shard_map(
        local,
        mesh=mesh,
        in_specs=placed,
        out_specs=(P("dp", "tensor"), P("tensor", None), P(None, "tensor")),
        check_vma=False,
    )
```

```python
import functools

import jax
import jax.numpy as jnp
from jax import lax
from jax.experimental import pallas as pl
from jax.experimental.pallas import tpu as pltpu
from jax.sharding import PartitionSpec as P

ADAPTER_SCALE = 2.0
EPSILON = 1e-06
F32, BF16 = jnp.float32, jnp.bfloat16
LANES = 128
ROWS = 256
WAIT = 5_000_000_000
VMEM = pl.BlockSpec(memory_space=pltpu.VMEM)
SMEM = pl.BlockSpec(memory_space=pltpu.SMEM)


def dot(a, b, dims=((1,), (0,))):
    return lax.dot_general(a, b, (dims, ((), ())), preferred_element_type=F32)


def call(body, outs, name, *args, near=(), far=(), keep=(), scratch=(), flops=0, limit=24):
    size = sum(a.size * a.dtype.itemsize for a in args + near + far)
    specs = [SMEM if a.dtype == jnp.int32 and a.size == 1 else VMEM for a in args]
    specs += [pl.BlockSpec(memory_space=pltpu.HBM)] * (len(near) + len(far)) + [VMEM] * len(keep)
    held = [pltpu.VMEM(a.shape, a.dtype) for a in near]
    held += [pltpu.SemaphoreType.DMA((len(near),))] if near else []

    def run(*refs):
        refs = list(refs)
        inputs = [refs.pop(0) for _ in args]
        distant = [refs.pop(0) for _ in near]
        inputs += [refs.pop(0) for _ in far]
        del refs[: len(keep)]
        if near:
            sems = refs.pop()
            here = refs[len(refs) - len(near) :]
            del refs[len(refs) - len(near) :]
            copies = [pltpu.make_async_copy(a, b, sems.at[i]) for i, (a, b) in enumerate(zip(distant, here))]
            for copy in copies:
                copy.start()
            inputs = (inputs, here, copies)
            body(inputs, *refs)
        else:
            body(*inputs, *refs)

    return pl.pallas_call(
        run,
        out_shape=[jax.ShapeDtypeStruct(*s) if isinstance(s, tuple) else s for s in outs],
        in_specs=specs,
        out_specs=[VMEM] * len(outs),
        scratch_shapes=list(scratch) + held,
        compiler_params=pltpu.CompilerParams(vmem_limit_bytes=limit << 20),
        cost_estimate=pl.CostEstimate(flops=flops, bytes_accessed=size, transcendentals=0),
        name=name,
    )(*args, *[pltpu.with_memory_space_constraint(a, pltpu.HBM) for a in near + far], *keep)


def cuts(total, step):
    return [(at, min(step, total - at)) for at in range(0, total, step)]


def iota(shape, dim):
    return lax.broadcasted_iota(jnp.int32, shape, dim)


def turned(column):
    n = column.shape[0]
    return jnp.sum(jnp.where(iota((n, n), 0) == iota((n, n), 1), column, 0), axis=0, keepdims=True)


def route_body(passes, capacity, inputs, out_ref, last_ref, mine_ref):
    (device_ref,), (index_ref, lengths_ref, table_ref), copies = inputs
    rows, slots = table_ref.shape[0], out_ref.shape[0]
    copies[0].wait()
    index = index_ref[...]
    total = index.shape[1]
    mine = device_ref[0] * rows + iota((rows, total), 0)
    packed = iota((rows, total), 1) // passes
    dest = jnp.sum(jnp.where(index == mine, packed, 0), axis=1, keepdims=True)
    earlier = (dest == turned(dest)) & (iota((rows, rows), 1) < iota((rows, rows), 0))
    rank = jnp.sum(earlier.astype(jnp.int32), axis=1, keepdims=True)
    slot = turned(dest * capacity + rank)
    picker = (iota((slots, rows), 0) == slot).astype(F32).astype(BF16)
    own = iota((passes, total), 1) == device_ref[0] * passes + iota((passes, total), 0)
    mine_ref[...] = jnp.sum(jnp.where(own, index, 0), axis=1, keepdims=True)
    copies[1].wait()
    upto = jnp.where(iota((passes, passes), 1) <= iota((passes, passes), 0), lengths_ref[...], 0)
    last_ref[...] = jnp.sum(upto, axis=1, keepdims=True) - 1
    copies[2].wait()
    out_ref[...] = dot(picker, table_ref[...]).astype(BF16)


def slot_picker(index_ref, owners, owned, capacity):
    column = index_ref[...]
    n = column.shape[0]
    row = turned(column)
    owner = column // owned
    earlier = (owner == row // owned) & (row < column)
    slot = owner * capacity + jnp.sum(earlier.astype(jnp.int32), axis=1, keepdims=True)
    return (slot == iota((n, owners * capacity), 1)).astype(F32).astype(BF16)


def project_body(inputs, out_ref, pooled_ref, low_ref, act_held, weight_held, act_sems, sems):
    (member_ref, last_ref, act_ref, weight_ref), (residual_ref, input_factor_ref), copies = inputs
    hidden = weight_held.shape[0]
    pieces = []
    for i, (at, size) in enumerate(cuts(hidden, ROWS)):
        piece = slice(at, at + size)
        act_copy = pltpu.make_async_copy(act_ref.at[:, piece], act_held.at[:, piece], act_sems.at[i])
        act_copy.start()
        copy = pltpu.make_async_copy(weight_ref.at[piece], weight_held.at[piece], sems.at[i])
        copy.start()
        pieces.append((piece, act_copy, copy))
    picker = (last_ref[...] == iota((last_ref.shape[0], act_ref.shape[0]), 1)).astype(F32).astype(BF16)
    for piece, act_copy, copy in pieces:
        act_copy.wait()
        pooled = dot(picker, act_held[:, piece]).astype(BF16)
        pooled_ref[:, piece] = pooled
        copy.wait()
        value = dot(pooled, weight_held[piece, :])
        if piece.start == 0:
            out_ref[...] = value
        else:
            out_ref[...] += value
    for copy in copies:
        copy.wait()
    low_ref[...] = dot(pooled_ref[...], input_factor_ref[...], ((1,), (1,)))
    columns = residual_ref.shape[1]
    own = pl.ds(pl.multiple_of(member_ref[0] * columns, LANES), columns)
    out_ref[:, own] += residual_ref[...].astype(F32)


def half_of(half, width, parts_ref, low_ref, factor_ref):
    columns = pl.ds(pl.multiple_of(half * width, LANES), width)
    return parts_ref[:, columns] + ADAPTER_SCALE * dot(low_ref[...].astype(BF16), factor_ref[:, columns])


def finish_body(owners, owned, capacity, member_ref, index_ref, routed_ref, parts_ref, low_ref, factor_ref, away_ref,
                grads_ref):
    width, rank = parts_ref.shape[1] // 2, low_ref.shape[1]
    away_ref[:, :width] = half_of(1 - member_ref[0] % 2, width, parts_ref, low_ref, factor_ref)
    away_ref[:, width:] = jnp.zeros_like(away_ref[:, width:])
    away_ref[:, width : width + rank] = low_ref[...]
    grads_ref[...] = dot(slot_picker(index_ref, owners, owned, capacity), routed_ref[...]).astype(BF16)


def put_low(low, at, out_ref):
    rank = low.shape[1]
    high = low.astype(BF16)
    out_ref[:, at:] = jnp.zeros_like(out_ref[:, at:])
    out_ref[:, at : at + rank] = high
    out_ref[:, at + rank : at + 2 * rank] = (low - high.astype(F32)).astype(BF16)


def sum_cores_body(member_ref, parts_ref, low_ref, away_ref, factor_ref, total_ref, low_total_ref, out_ref):
    width, rank = parts_ref.shape[1] // 2, low_ref.shape[1]
    total = half_of(member_ref[0] % 2, width, parts_ref, low_ref, factor_ref) + away_ref[:, :width]
    low = low_ref[...] + away_ref[:, width : width + rank]
    total_ref[...] = total
    low_total_ref[...] = low
    out_ref[:, :width] = total.astype(BF16)
    put_low(low, width, out_ref)


def sum_chips_body(last, total_ref, low_ref, got_ref, grads_ref, got_grads_ref, new_total_ref, new_low_ref, out_ref,
                   *more):
    width, rank = total_ref.shape[1], low_ref.shape[1]
    total = total_ref[...] + got_ref[:, :width].astype(F32)
    low = low_ref[...]
    for i in range(2):
        low += got_ref[:, width + i * rank : width + (i + 1) * rank].astype(F32)
    new_total_ref[...] = total
    new_low_ref[...] = low
    out_ref[:, :width] = total.astype(BF16)
    columns = grads_ref.shape[1]
    if last:
        joined_ref, at = out_ref, width
    else:
        put_low(low, width, out_ref)
        (joined_ref,), at = more, 0
    joined_ref[:, at : at + columns] = grads_ref[...]
    joined_ref[:, at + columns : at + 2 * columns] = got_grads_ref[...]


def direction_body(count, blocks, member_ref, total_ref, low_ref, mine_ref, other_ref, factor_ref, pooled_ref,
                   direction_ref, spread_ref, packed_ref):
    member = member_ref[0]
    width = total_ref.shape[1]
    columns = width // blocks

    def hidden_block(b):
        piece = slice(b % blocks * columns, (b % blocks + 1) * columns)
        return jnp.where(member % 2 == b // blocks, total_ref[:, piece], other_ref[:, piece].astype(F32))

    def grads_block(b):
        apart = member ^ b
        piece = pl.ds(pl.multiple_of(width + apart // 2 * columns, LANES), columns)
        return jnp.where(apart % 2 == 0, mine_ref[:, piece].astype(F32), other_ref[:, piece].astype(F32))

    squares = sum(jnp.sum(hidden_block(b) ** 2, axis=1, keepdims=True) for b in range(2 * blocks))
    length = jnp.sqrt(squares + EPSILON)
    along = sum(
        jnp.sum(grads_block(b) * (hidden_block(b) / length), axis=1, keepdims=True) for b in range(2 * blocks)
    )
    for b in range(2 * blocks):
        value = (grads_block(b) - along * (hidden_block(b) / length)) / length
        direction_ref[:, b * columns : (b + 1) * columns] = value.astype(BF16)
    spread = dot(direction_ref[...], factor_ref[...], ((1,), (1,))).astype(BF16)
    spread_ref[...] = spread
    hidden = pooled_ref.shape[1]
    scale = ADAPTER_SCALE / count
    packed_ref[:, :hidden] = (scale * dot(spread, pooled_ref[...], ((0,), (0,)))).astype(BF16)
    own = direction_ref[:, pl.ds(pl.multiple_of(member * columns, LANES), columns)]
    packed_ref[:, hidden:] = (scale * dot(low_ref[...].astype(BF16), own, ((0,), (0,)))).astype(BF16)


def round_sum_body(own_ref, got_ref, *refs):
    refs[-1][...] = (own_ref[...].astype(F32) + got_ref[...].astype(F32)).astype(BF16)


def last_sum_body(own_ref, got_ref, *refs):
    first_ref, second_ref = refs[-2:]
    total = own_ref[...].astype(F32) + got_ref[...].astype(F32)
    hidden = first_ref.shape[1]
    first_ref[...] = total[:, :hidden]
    second_ref[...] = total[:, hidden:]


def activation_body(start, stop, direction_ref, spread_ref, input_factor_ref, weight_ref, *refs):
    *before, out_ref, token_ref = refs
    token_ref[...] = jnp.zeros_like(token_ref)
    for ref in before:
        out_ref[:, :start] = ref[:, :start]

    def part(at, size):
        columns = pl.ds(at, size)
        value = ADAPTER_SCALE * dot(spread_ref[...], input_factor_ref[:, columns])
        value += dot(direction_ref[...], weight_ref[columns, :], ((1,), (1,)))
        out_ref[:, columns] = value.astype(BF16)

    whole = (stop - start) // ROWS

    @pl.loop(0, whole)
    def _(i):
        part(pl.multiple_of(start + i * ROWS, ROWS), ROWS)

    if whole * ROWS < stop - start:
        part(start + whole * ROWS, stop - start - whole * ROWS)


def local(gradient_table, residual_input_rows, act, down_weight, adapter_input_factor, adapter_output_factor, lengths,
          owning_row_index):
    devices = lax.axis_size("dp")
    members = lax.axis_size("tensor")
    device = lax.axis_index("dp")
    member = lax.axis_index("tensor")
    passes = lengths.shape[1]
    owned, columns = gradient_table.shape
    rank, model = adapter_output_factor.shape
    hidden = act.shape[1]
    capacity = -(-passes // devices)
    slots = devices * capacity
    blocks = members // 2
    width = blocks * columns
    count = passes * devices
    dp_at = device.astype(jnp.int32).reshape(1)
    member_at = member.astype(jnp.int32).reshape(1)
    input_factor = adapter_input_factor.T

    def swap(x, axis, size, bit):
        return lax.ppermute(x, axis, [(i, i ^ bit) for i in range(size)])

    steps = []
    bit = 2
    while bit < members:
        steps.append(bit)
        bit *= 2

    index = owning_row_index.reshape(1, -1)
    sent, last, my_index = call(
        functools.partial(route_body, passes, capacity),
        [((slots, columns), BF16), ((passes, 1), jnp.int32), ((passes, 1), jnp.int32)], "route",
        dp_at, near=(index, lengths, gradient_table),
    )
    routed = lax.all_to_all(sent, "dp", 0, 0, tiled=True)
    pieces = len(cuts(hidden, ROWS))
    terms, pooled, low = call(
        project_body, [((passes, model), F32), ((passes, hidden), BF16), ((passes, rank), F32)], "project",
        member_at, last, near=(residual_input_rows, input_factor), far=(act, down_weight),
        scratch=[pltpu.VMEM(act.shape, BF16), pltpu.VMEM(down_weight.shape, BF16)]
        + [pltpu.SemaphoreType.DMA((pieces,))] * 2,
        flops=2 * passes * hidden * model,
    )
    away, grads = call(
        functools.partial(finish_body, devices, owned, capacity),
        [((passes, width + LANES), F32), ((passes, columns), BF16)], "finish",
        member_at, my_index, routed, terms, low, adapter_output_factor,
    )
    away = swap(away, "tensor", members, 1)
    sums = [((passes, width), F32), ((passes, rank), F32)]
    total, low, out = call(
        sum_cores_body, [*sums, ((passes, width + LANES), BF16)], "sum_cores",
        member_at, terms, low, away, adapter_output_factor,
    )
    weight = pltpu.with_memory_space_constraint(down_weight, pltpu.VMEM)
    for bit in steps:
        got, got_grads = swap(out, "tensor", members, bit), swap(grads, "tensor", members, bit)
        joined = 2 * grads.shape[1]
        last = bit == steps[-1]
        outs = [((passes, width + joined), BF16)] if last else [(out.shape, BF16), ((passes, joined), BF16)]
        total, low, out, *more = call(
            functools.partial(sum_chips_body, last), [*sums, *outs], "sum_chips",
            total, low, got, grads, got_grads, flops=WAIT,
        )
        grads = more[0] if more else None
    other = swap(out, "tensor", members, 1)
    direction, spread, packed = call(
        functools.partial(direction_body, count, blocks),
        [((passes, model), BF16), ((passes, rank), BF16), ((rank, hidden + columns), BF16)], "direction",
        member_at, total, low, out, other, adapter_output_factor, pooled, flops=WAIT,
    )
    parts = 3
    ends = [min(hidden, -(-pieces * (i + 1) // parts) * ROWS) for i in range(parts)]
    token = []
    activation = []

    def activate():
        start = ends[len(ends) - len(todo) - 1] if len(todo) < parts else 0
        stop = todo.pop(0)
        out, done = call(
            functools.partial(activation_body, start, stop), [((passes, hidden), BF16), ((8, LANES), F32)], "activation",
            direction, spread, input_factor, weight, *activation,
            flops=passes * (stop - start) * model * 2,
        )
        activation[:] = [out]
        token[:] = [done]

    todo = list(ends)
    shapes = [((rank, hidden), F32), ((rank, columns), F32)]
    if devices & (devices - 1) == 0:
        bit = 1
        while bit < devices:
            got = swap(packed, "dp", devices, bit)
            bit *= 2
            if todo:
                activate()
            if bit < devices:
                (packed,) = call(round_sum_body, [(packed.shape, BF16)], "sum_pairs", packed, got, *token, keep=(weight,))
            else:
                sums = call(last_sum_body, shapes, "sum_last", packed, got, *token)
    else:
        packed = lax.psum(packed.astype(F32), "dp")
        sums = packed[:, :hidden], packed[:, hidden:]
    while todo:
        activate()
    return activation[0], sums[0].T, sums[1]


def solution(mesh):
    placed = (
        P("dp", "tensor"),
        P("dp", "tensor"),
        P("dp", "tensor"),
        P("tensor", None),
        P("tensor", None),
        P(),
        P("dp", None),
        P(),
    )
    return jax.shard_map(
        local,
        mesh=mesh,
        in_specs=placed,
        out_specs=(P("dp", "tensor"), P("tensor", None), P(None, "tensor")),
        check_vma=False,
    )
```

```python
import functools

import jax
import jax.numpy as jnp
from jax import lax
from jax.experimental import pallas as pl
from jax.experimental.pallas import tpu as pltpu
from jax.sharding import PartitionSpec as P

ADAPTER_SCALE = 2.0
EPSILON = 1e-06
F32, BF16 = jnp.float32, jnp.bfloat16
LANES = 128
ROWS = 256
WAIT = 5_000_000_000
VMEM = pl.BlockSpec(memory_space=pltpu.VMEM)
SMEM = pl.BlockSpec(memory_space=pltpu.SMEM)


def dot(a, b, dims=((1,), (0,))):
    return lax.dot_general(a, b, (dims, ((), ())), preferred_element_type=F32)


def call(body, outs, name, *args, near=(), far=(), keep=(), scratch=(), flops=0, limit=24):
    size = sum(a.size * a.dtype.itemsize for a in args + near + far)
    specs = [SMEM if a.dtype == jnp.int32 and a.size == 1 else VMEM for a in args]
    specs += [pl.BlockSpec(memory_space=pltpu.HBM)] * (len(near) + len(far)) + [VMEM] * len(keep)
    held = [pltpu.VMEM(a.shape, a.dtype) for a in near]
    held += [pltpu.SemaphoreType.DMA((len(near),))] if near else []

    def run(*refs):
        refs = list(refs)
        inputs = [refs.pop(0) for _ in args]
        distant = [refs.pop(0) for _ in near]
        inputs += [refs.pop(0) for _ in far]
        del refs[: len(keep)]
        if near:
            sems = refs.pop()
            here = refs[len(refs) - len(near) :]
            del refs[len(refs) - len(near) :]
            copies = [pltpu.make_async_copy(a, b, sems.at[i]) for i, (a, b) in enumerate(zip(distant, here))]
            for copy in copies:
                copy.start()
            inputs = (inputs, here, copies)
            body(inputs, *refs)
        else:
            body(*inputs, *refs)

    return pl.pallas_call(
        run,
        out_shape=[jax.ShapeDtypeStruct(*s) if isinstance(s, tuple) else s for s in outs],
        in_specs=specs,
        out_specs=[VMEM] * len(outs),
        scratch_shapes=list(scratch) + held,
        compiler_params=pltpu.CompilerParams(vmem_limit_bytes=limit << 20),
        cost_estimate=pl.CostEstimate(flops=flops, bytes_accessed=size, transcendentals=0),
        name=name,
    )(*args, *[pltpu.with_memory_space_constraint(a, pltpu.HBM) for a in near + far], *keep)


def cuts(total, step):
    return [(at, min(step, total - at)) for at in range(0, total, step)]


def iota(shape, dim):
    return lax.broadcasted_iota(jnp.int32, shape, dim)


def turned(column):
    n = column.shape[0]
    return jnp.sum(jnp.where(iota((n, n), 0) == iota((n, n), 1), column, 0), axis=0, keepdims=True)


def route_body(passes, capacity, inputs, out_ref, last_ref, mine_ref):
    (device_ref,), (index_ref, lengths_ref, table_ref), copies = inputs
    rows, slots = table_ref.shape[0], out_ref.shape[0]
    copies[0].wait()
    index = index_ref[...]
    total = index.shape[1]
    mine = device_ref[0] * rows + iota((rows, total), 0)
    packed = iota((rows, total), 1) // passes
    dest = jnp.sum(jnp.where(index == mine, packed, 0), axis=1, keepdims=True)
    earlier = (dest == turned(dest)) & (iota((rows, rows), 1) < iota((rows, rows), 0))
    rank = jnp.sum(earlier.astype(jnp.int32), axis=1, keepdims=True)
    slot = turned(dest * capacity + rank)
    picker = (iota((slots, rows), 0) == slot).astype(F32).astype(BF16)
    own = iota((passes, total), 1) == device_ref[0] * passes + iota((passes, total), 0)
    mine_ref[...] = jnp.sum(jnp.where(own, index, 0), axis=1, keepdims=True)
    copies[1].wait()
    upto = jnp.where(iota((passes, passes), 1) <= iota((passes, passes), 0), lengths_ref[...], 0)
    last_ref[...] = jnp.sum(upto, axis=1, keepdims=True) - 1
    copies[2].wait()
    out_ref[...] = dot(picker, table_ref[...]).astype(BF16)


def slot_picker(index_ref, owners, owned, capacity):
    column = index_ref[...]
    n = column.shape[0]
    row = turned(column)
    owner = column // owned
    earlier = (owner == row // owned) & (row < column)
    slot = owner * capacity + jnp.sum(earlier.astype(jnp.int32), axis=1, keepdims=True)
    return (slot == iota((n, owners * capacity), 1)).astype(F32).astype(BF16)


def project_body(inputs, out_ref, pooled_ref, low_ref, act_held, weight_held, act_sems, sems):
    (member_ref, last_ref, act_ref, weight_ref), (residual_ref, input_factor_ref), copies = inputs
    hidden = weight_held.shape[0]
    pieces = []
    for i, (at, size) in enumerate(cuts(hidden, ROWS)):
        piece = slice(at, at + size)
        act_copy = pltpu.make_async_copy(act_ref.at[:, piece], act_held.at[:, piece], act_sems.at[i])
        act_copy.start()
        copy = pltpu.make_async_copy(weight_ref.at[piece], weight_held.at[piece], sems.at[i])
        copy.start()
        pieces.append((piece, act_copy, copy))
    picker = (last_ref[...] == iota((last_ref.shape[0], act_ref.shape[0]), 1)).astype(F32).astype(BF16)
    for piece, act_copy, copy in pieces:
        act_copy.wait()
        pooled = dot(picker, act_held[:, piece]).astype(BF16)
        pooled_ref[:, piece] = pooled
        copy.wait()
        value = dot(pooled, weight_held[piece, :])
        if piece.start == 0:
            out_ref[...] = value
        else:
            out_ref[...] += value
    for copy in copies:
        copy.wait()
    low_ref[...] = dot(pooled_ref[...], input_factor_ref[...], ((1,), (1,)))
    columns = residual_ref.shape[1]
    own = pl.ds(pl.multiple_of(member_ref[0] * columns, LANES), columns)
    out_ref[:, own] += residual_ref[...].astype(F32)


def term_of(block, columns, parts_ref, low_ref, factor_ref):
    at = pl.ds(pl.multiple_of(block * columns, LANES), columns)
    return parts_ref[:, at] + ADAPTER_SCALE * dot(low_ref[...].astype(BF16), factor_ref[:, at])


def finish_body(owners, owned, capacity, member_ref, index_ref, routed_ref, parts_ref, low_ref, factor_ref, away_ref,
                grads_ref):
    columns = grads_ref.shape[1]
    for j in range(away_ref.shape[1] // columns):
        block = 2 * j + 1 - member_ref[0] % 2
        away_ref[:, j * columns : (j + 1) * columns] = term_of(block, columns, parts_ref, low_ref, factor_ref)
    grads_ref[...] = dot(slot_picker(index_ref, owners, owned, capacity), routed_ref[...]).astype(BF16)


def sum_cores_body(columns, member_ref, parts_ref, low_ref, away_ref, factor_ref, pooled_ref, keep_ref, send_ref,
                   pooled_out_ref):
    pooled_out_ref[...] = pooled_ref[...]
    member = member_ref[0]
    n = keep_ref.shape[1] // columns
    side = member // 2 // n % 2
    for i in range(n):
        for ref, j in ((keep_ref, side * n + i), (send_ref, (1 - side) * n + i)):
            value = term_of(2 * j + member % 2, columns, parts_ref, low_ref, factor_ref)
            value += away_ref[:, pl.ds(pl.multiple_of(j * columns, LANES), columns)]
            ref[:, i * columns : (i + 1) * columns] = value.astype(ref.dtype)


def sum_chips_body(columns, member_ref, kept_ref, got_ref, keep_ref, send_ref):
    n = keep_ref.shape[1] // columns
    side = member_ref[0] // 2 // n % 2
    for ref, half in ((keep_ref, side), (send_ref, 1 - side)):
        at = pl.ds(pl.multiple_of(half * n * columns, LANES), n * columns)
        ref[...] = (kept_ref[:, at] + got_ref[:, at].astype(F32)).astype(ref.dtype)


def stats_body(member_ref, kept_ref, got_ref, grads_ref, low_ref, factor_ref, hidden_ref, stats_ref):
    rank = low_ref.shape[1]
    columns = grads_ref.shape[1]
    hidden = kept_ref[...] + got_ref[...].astype(F32)
    hidden_ref[...] = hidden
    factor = factor_ref[:, pl.ds(pl.multiple_of(member_ref[0] * columns, LANES), columns)]
    high = hidden.astype(BF16)
    rest = (hidden - high.astype(F32)).astype(BF16)
    lanes = ((1,), (1,))
    stats_ref[...] = jnp.zeros_like(stats_ref)
    stats_ref[:, :1] = jnp.sum(hidden * hidden, axis=1, keepdims=True)
    stats_ref[:, 1:2] = jnp.sum(hidden * grads_ref[...].astype(F32), axis=1, keepdims=True)
    stats_ref[:, rank : 2 * rank] = dot(high, factor, lanes) + dot(rest, factor, lanes)
    stats_ref[:, 2 * rank : 3 * rank] = dot(grads_ref[...], factor, lanes)
    stats_ref[:, 3 * rank : 4 * rank] = low_ref[...]


def direction_body(count, stats_ref, got_ref, hidden_ref, grads_ref, direction_ref, spread_ref, packed_ref):
    rank = spread_ref.shape[1]
    stats = stats_ref[...] + got_ref[...]
    length = jnp.sqrt(stats[:, :1] + EPSILON)
    along = stats[:, 1:2] / length
    direction = ((grads_ref[...].astype(F32) - along * (hidden_ref[...] / length)) / length).astype(BF16)
    direction_ref[...] = direction
    spread = (stats[:, 2 * rank : 3 * rank] - along * (stats[:, rank : 2 * rank] / length)) / length
    spread = spread.astype(BF16)
    spread_ref[...] = spread
    low = stats[:, 3 * rank : 4 * rank].astype(BF16)
    passes, columns = direction.shape
    packed_ref[:, :columns] = (ADAPTER_SCALE / count * dot(low, direction, ((0,), (0,)))).astype(BF16)
    packed_ref[:, columns:] = jnp.zeros_like(packed_ref[:, columns:])
    same = (iota((passes, passes), 0) == iota((passes, passes), 1)).astype(F32).astype(BF16)
    packed_ref[:, columns : columns + passes] = dot(spread, same, ((0,), (0,))).astype(BF16)


def first_sum_body(count, columns, sides, *refs):
    packed, pooled, out_ref = refs[:sides], refs[sides : 2 * sides], refs[-1]
    hidden = out_ref.shape[1] - columns
    passes = pooled[0].shape[0]
    first = sum(dot(a[:, columns : columns + passes], b[...]) for a, b in zip(packed, pooled))
    out_ref[:, :hidden] = (ADAPTER_SCALE / count * first).astype(BF16)
    out_ref[:, hidden:] = sum(a[:, :columns].astype(F32) for a in packed).astype(BF16)


def round_sum_body(own_ref, got_ref, *refs):
    refs[-1][...] = (own_ref[...].astype(F32) + got_ref[...].astype(F32)).astype(BF16)


def last_sum_body(own_ref, got_ref, *refs):
    first_ref, second_ref = refs[-2:]
    total = own_ref[...].astype(F32) + got_ref[...].astype(F32)
    hidden = first_ref.shape[1]
    first_ref[...] = total[:, :hidden]
    second_ref[...] = total[:, hidden:]


def activation_body(masks, first, member_ref, weight_ref, *refs):
    *before, out_ref, token_ref = refs
    pieces = [before.pop() for _ in masks][::-1]
    token_ref[...] = jnp.zeros_like(token_ref)
    columns = pieces[0].shape[1]

    def part(at, size):
        rows = pl.ds(at, size)
        if first:
            value = ADAPTER_SCALE * dot(before[0][...], before[1][:, rows])
        else:
            value = before[0][:, rows]
        for mask, piece in zip(masks, pieces):
            block = pl.ds(pl.multiple_of((member_ref[0] ^ mask) * columns, LANES), columns)
            value += dot(piece[...], weight_ref[rows, block], ((1,), (1,)))
        out_ref[:, rows] = value.astype(out_ref.dtype)

    total = out_ref.shape[1]

    @pl.loop(0, total // ROWS)
    def _(i):
        part(pl.multiple_of(i * ROWS, ROWS), ROWS)

    if total % ROWS:
        part(total - total % ROWS, total % ROWS)


def local(gradient_table, residual_input_rows, act, down_weight, adapter_input_factor, adapter_output_factor, lengths,
          owning_row_index):
    devices = lax.axis_size("dp")
    members = lax.axis_size("tensor")
    device = lax.axis_index("dp")
    member = lax.axis_index("tensor")
    passes = lengths.shape[1]
    owned, columns = gradient_table.shape
    rank, model = adapter_output_factor.shape
    hidden = act.shape[1]
    capacity = -(-passes // devices)
    slots = devices * capacity
    blocks = members // 2
    width = blocks * columns
    count = passes * devices
    dp_at = device.astype(jnp.int32).reshape(1)
    member_at = member.astype(jnp.int32).reshape(1)
    input_factor = adapter_input_factor.T

    def swap(x, axis, size, bit):
        return lax.ppermute(x, axis, [(i, i ^ bit) for i in range(size)])

    index = owning_row_index.reshape(1, -1)
    sent, last, my_index = call(
        functools.partial(route_body, passes, capacity),
        [((slots, columns), BF16), ((passes, 1), jnp.int32), ((passes, 1), jnp.int32)], "route",
        dp_at, near=(index, lengths, gradient_table),
    )
    routed = lax.all_to_all(sent, "dp", 0, 0, tiled=True)
    pieces = len(cuts(hidden, ROWS))
    terms, pooled, low = call(
        project_body, [((passes, model), F32), ((passes, hidden), BF16), ((passes, rank), F32)], "project",
        member_at, last, near=(residual_input_rows, input_factor), far=(act, down_weight),
        scratch=[pltpu.VMEM(act.shape, BF16), pltpu.VMEM(down_weight.shape, BF16)]
        + [pltpu.SemaphoreType.DMA((pieces,))] * 2,
        flops=2 * passes * hidden * model,
    )
    away, grads = call(
        functools.partial(finish_body, devices, owned, capacity),
        [((passes, blocks * columns), F32), ((passes, columns), BF16)], "finish",
        member_at, my_index, routed, terms, low, adapter_output_factor,
    )
    away = swap(away, "tensor", members, 1)
    n = blocks // 2
    kept, out, pooled = call(
        functools.partial(sum_cores_body, columns),
        [((passes, n * columns), F32), ((passes, n * columns), BF16), (pooled.shape, BF16)],
        "sum_cores", member_at, terms, low, away, adapter_output_factor, pooled,
    )
    paired = devices & (devices - 1) == 0
    far = [swap(pooled, "dp", devices, devices // 2)] if paired else []
    got = swap(out, "tensor", members, 2 * n)
    while n > 1:
        n //= 2
        kept, out = call(
            functools.partial(sum_chips_body, columns), [((passes, n * columns), F32), ((passes, n * columns), BF16)],
            "sum_chips", member_at, kept, got,
        )
        got = swap(out, "tensor", members, 2 * n)
    hidden_rows, stats = call(
        stats_body, [((passes, columns), F32), ((passes, LANES), F32)], "stats",
        member_at, kept, got, grads, low, adapter_output_factor, flops=2 * WAIT,
    )
    bit = 1
    while 2 * bit < members:
        stats = stats + swap(stats, "tensor", members, bit)
        bit *= 2
    got = swap(stats, "tensor", members, bit)
    direction, spread, packed = call(
        functools.partial(direction_body, count),
        [((passes, columns), BF16), ((passes, rank), BF16), ((rank, columns + LANES * -(-passes // LANES)), BF16)],
        "direction", stats, got, hidden_rows, grads, flops=passes * columns * 64,
    )
    directions = {0: direction}
    bit = 2
    while bit < members:
        directions.update({k ^ bit: swap(v, "tensor", members, bit) for k, v in list(directions.items())})
        bit *= 2
    directions.update({k ^ 1: swap(v, "tensor", members, 1) for k, v in list(directions.items())})
    weight = pltpu.with_memory_space_constraint(down_weight, pltpu.VMEM)
    order = list(range(members))
    todo = [order[:1], order[1:-1], order[-1:]]
    token, activation = [], []

    def activate():
        masks = todo.pop(0)
        out, done = call(
            functools.partial(activation_body, masks, not activation),
            [((passes, hidden), F32 if todo else BF16), ((8, LANES), F32)], "activation",
            member_at, weight, *(activation or (spread, input_factor)), *[directions[k] for k in masks],
            flops=2 * passes * hidden * columns * len(masks),
        )
        activation[:] = [out]
        token[:] = [done]

    shapes = [((rank, hidden), F32), ((rank, columns), F32)]
    both = [((rank, hidden + columns), BF16)]
    first = functools.partial(first_sum_body, count, columns)
    if paired:
        got = swap(packed, "dp", devices, devices // 2)
        activate()
        (packed,) = call(functools.partial(first, 2), both, "sum_far", packed, got, pooled, *far, *token, keep=(weight,))
        bit = 1
        while bit < devices // 2:
            got = swap(packed, "dp", devices, bit)
            bit *= 2
            if todo:
                activate()
            if bit < devices // 2:
                (packed,) = call(round_sum_body, both, "sum_pairs", packed, got, *token, keep=(weight,))
            else:
                sums = call(last_sum_body, shapes, "sum_last", packed, got, *token)
    else:
        (packed,) = call(functools.partial(first, 1), both, "sum_own", packed, pooled)
        packed = lax.psum(packed.astype(F32), "dp")
        sums = packed[:, :hidden], packed[:, hidden:]
    while todo:
        activate()
    return activation[0], sums[0].T, sums[1]


def solution(mesh):
    placed = (
        P("dp", "tensor"),
        P("dp", "tensor"),
        P("dp", "tensor"),
        P("tensor", None),
        P("tensor", None),
        P(),
        P("dp", None),
        P(),
    )
    return jax.shard_map(
        local,
        mesh=mesh,
        in_specs=placed,
        out_specs=(P("dp", "tensor"), P("tensor", None), P(None, "tensor")),
        check_vma=False,
    )
```

```python
import functools

import jax
import jax.numpy as jnp
from jax import lax
from jax.experimental import pallas as pl
from jax.experimental.pallas import tpu as pltpu
from jax.sharding import PartitionSpec as P

ADAPTER_SCALE = 2.0
EPSILON = 1e-06
F32, BF16 = jnp.float32, jnp.bfloat16
LANES = 128
ROWS = 256
STEP = 512
WAIT = 5_000_000_000
VMEM = pl.BlockSpec(memory_space=pltpu.VMEM)
SMEM = pl.BlockSpec(memory_space=pltpu.SMEM)


def dot(a, b, dims=((1,), (0,))):
    return lax.dot_general(a, b, (dims, ((), ())), preferred_element_type=F32)


def call(body, outs, name, *args, near=(), far=(), keep=(), scratch=(), flops=0, limit=24):
    size = sum(a.size * a.dtype.itemsize for a in args + near + far)
    specs = [SMEM if a.dtype == jnp.int32 and a.size == 1 else VMEM for a in args]
    specs += [pl.BlockSpec(memory_space=pltpu.HBM)] * (len(near) + len(far)) + [VMEM] * len(keep)
    held = [pltpu.VMEM(a.shape, a.dtype) for a in near]
    held += [pltpu.SemaphoreType.DMA((len(near),))] if near else []

    def run(*refs):
        refs = list(refs)
        inputs = [refs.pop(0) for _ in args]
        distant = [refs.pop(0) for _ in near]
        inputs += [refs.pop(0) for _ in far]
        del refs[: len(keep)]
        if near:
            sems = refs.pop()
            here = refs[len(refs) - len(near) :]
            del refs[len(refs) - len(near) :]
            copies = [pltpu.make_async_copy(a, b, sems.at[i]) for i, (a, b) in enumerate(zip(distant, here))]
            for copy in copies:
                copy.start()
            inputs = (inputs, here, copies)
            body(inputs, *refs)
        else:
            body(*inputs, *refs)

    return pl.pallas_call(
        run,
        out_shape=[jax.ShapeDtypeStruct(*s) if isinstance(s, tuple) else s for s in outs],
        in_specs=specs,
        out_specs=[VMEM] * len(outs),
        scratch_shapes=list(scratch) + held,
        compiler_params=pltpu.CompilerParams(vmem_limit_bytes=limit << 20),
        cost_estimate=pl.CostEstimate(flops=flops, bytes_accessed=size, transcendentals=0),
        name=name,
    )(*args, *[pltpu.with_memory_space_constraint(a, pltpu.HBM) for a in near + far], *keep)


def cuts(total, step):
    return [(at, min(step, total - at)) for at in range(0, total, step)]


def iota(shape, dim):
    return lax.broadcasted_iota(jnp.int32, shape, dim)


def turned(column):
    n = column.shape[0]
    return jnp.sum(jnp.where(iota((n, n), 0) == iota((n, n), 1), column, 0), axis=0, keepdims=True)


def apart(device, other):
    return device % 2 ^ other % 2, (device // 2) ^ (other // 2)


def route_body(passes, capacity, paired, inputs, *refs):
    (device_ref,), (index_ref, lengths_ref, table_ref), copies = inputs
    *out_refs, last_ref, mine_ref = refs
    rows, slots = table_ref.shape[0], sum(ref.shape[0] for ref in out_refs)
    device = device_ref[0]
    copies[0].wait()
    index = index_ref[...]
    total = index.shape[1]
    mine = device * rows + iota((rows, total), 0)
    packed = iota((rows, total), 1) // passes
    dest = jnp.sum(jnp.where(index == mine, packed, 0), axis=1, keepdims=True)
    earlier = (dest == turned(dest)) & (iota((rows, rows), 1) < iota((rows, rows), 0))
    rank = jnp.sum(earlier.astype(jnp.int32), axis=1, keepdims=True)
    place = dest
    if paired:
        low, high = apart(dest, device)
        place = 2 * high + low
    slot = turned(place * capacity + rank)
    picker = (iota((slots, rows), 0) == slot).astype(F32).astype(BF16)
    own = iota((passes, total), 1) == device * passes + iota((passes, total), 0)
    mine_ref[...] = jnp.sum(jnp.where(own, index, 0), axis=1, keepdims=True)
    copies[1].wait()
    upto = jnp.where(iota((passes, passes), 1) <= iota((passes, passes), 0), lengths_ref[...], 0)
    last_ref[...] = jnp.sum(upto, axis=1, keepdims=True) - 1
    copies[2].wait()
    value = dot(picker, table_ref[...]).astype(BF16)
    size = slots // len(out_refs)
    for i, ref in enumerate(out_refs):
        ref[...] = value[i * size : (i + 1) * size]


def meet_body(capacity, away_ref, *refs):
    *blocks, out_ref, keep_ref, send_ref = refs
    out_ref[...] = away_ref[...].astype(BF16)
    rows = jnp.concatenate([ref[...] for ref in blocks], axis=0)
    n, total = keep_ref.shape[0], rows.shape[0]
    to, at = iota((n, total), 0), iota((n, total), 1)
    for low, ref in ((0, keep_ref), (1, send_ref)):
        picker = (at == (2 * (to // capacity) + low) * capacity + to % capacity).astype(F32).astype(BF16)
        ref[...] = dot(picker, rows).astype(BF16)


def project_body(inputs, kept_ref, away_ref, pooled_ref, low_ref, act_held, weight_held, act_sems, sems):
    (member_ref, last_ref, act_ref, weight_ref), (input_factor_ref, factor_ref, residual_ref), copies = inputs
    member = member_ref[0]
    columns = residual_ref.shape[1]
    hidden = act_ref.shape[1]
    pieces = []
    for i, (at, size) in enumerate(cuts(hidden, ROWS)):
        piece = slice(at, at + size)
        act_copy = pltpu.make_async_copy(act_ref.at[:, piece], act_held.at[:, piece], act_sems.at[i])
        act_copy.start()
        copy = pltpu.make_async_copy(weight_ref.at[piece], weight_held.at[piece], sems.at[i])
        copy.start()
        pieces.append((piece, act_copy, copy))
    picker = (last_ref[...] == iota((last_ref.shape[0], act_ref.shape[0]), 1)).astype(F32).astype(BF16)

    def places():
        for ref, core in ((away_ref, 1 - member % 2), (kept_ref, member % 2)):
            for j in range(ref.shape[1] // columns):
                start = pl.multiple_of((2 * j + core) * columns, LANES)
                yield ref, slice(j * columns, (j + 1) * columns), pl.ds(start, columns)

    for piece, act_copy, copy in pieces:
        act_copy.wait()
        pooled = dot(picker, act_held[:, piece]).astype(BF16)
        pooled_ref[:, piece] = pooled
        copy.wait()
        for ref, to, at in places():
            value = dot(pooled, weight_held[piece, at])
            if piece.start == 0:
                ref[:, to] = value
            else:
                ref[:, to] += value
    for copy in copies:
        copy.wait()
    low = dot(pooled_ref[...], input_factor_ref[...], ((1,), (1,)))
    low_ref[...] = low
    for ref, to, at in places():
        ref[:, to] += ADAPTER_SCALE * dot(low.astype(BF16), factor_ref[:, at])
    own = pl.ds(pl.multiple_of(member // 2 * columns, LANES), columns)
    kept_ref[:, own] += residual_ref[...].astype(F32)


def round_body(away_ref, out_ref):
    out_ref[...] = away_ref[...].astype(BF16)


def grads_body(owned, capacity, device_ref, index_ref, *refs):
    *parts, grads_ref = refs
    column = index_ref[...]
    row = turned(column)
    owner = column // owned
    earlier = (owner == row // owned) & (row < column)
    rank = jnp.sum(earlier.astype(jnp.int32), axis=1, keepdims=True)
    slots = parts[0].shape[0]
    low = jnp.zeros_like(owner)
    place = owner
    if len(parts) == 2:
        low, place = apart(owner, device_ref[0])
    total = 0
    for i, part in enumerate(parts):
        picker = (low == i) & (place * capacity + rank == iota((column.shape[0], slots), 1))
        total += dot(picker.astype(F32).astype(BF16), part[...])
    grads_ref[...] = total.astype(BF16)


def sum_cores_body(columns, member_ref, kept_ref, away_ref, pooled_ref, keep_ref, send_ref, pooled_out_ref):
    pooled_out_ref[...] = pooled_ref[...]
    n = keep_ref.shape[1] // columns
    side = member_ref[0] // 2 // n % 2
    for ref, half in ((keep_ref, side), (send_ref, 1 - side)):
        at = pl.ds(pl.multiple_of(half * n * columns, LANES), n * columns)
        ref[...] = (kept_ref[:, at] + away_ref[:, at].astype(F32)).astype(ref.dtype)


def sum_chips_body(columns, member_ref, kept_ref, got_ref, keep_ref, send_ref):
    n = keep_ref.shape[1] // columns
    side = member_ref[0] // 2 // n % 2
    for ref, half in ((keep_ref, side), (send_ref, 1 - side)):
        at = pl.ds(pl.multiple_of(half * n * columns, LANES), n * columns)
        ref[...] = (kept_ref[:, at] + got_ref[:, at].astype(F32)).astype(ref.dtype)


def stats_body(member_ref, kept_ref, got_ref, grads_ref, low_ref, factor_ref, hidden_ref, stats_ref):
    rank = low_ref.shape[1]
    columns = grads_ref.shape[1]
    hidden = kept_ref[...] + got_ref[...].astype(F32)
    hidden_ref[...] = hidden
    factor = factor_ref[:, pl.ds(pl.multiple_of(member_ref[0] * columns, LANES), columns)]
    high = hidden.astype(BF16)
    rest = (hidden - high.astype(F32)).astype(BF16)
    lanes = ((1,), (1,))
    stats_ref[...] = jnp.zeros_like(stats_ref)
    stats_ref[:, :1] = jnp.sum(hidden * hidden, axis=1, keepdims=True)
    stats_ref[:, 1:2] = jnp.sum(hidden * grads_ref[...].astype(F32), axis=1, keepdims=True)
    stats_ref[:, rank : 2 * rank] = dot(high, factor, lanes) + dot(rest, factor, lanes)
    stats_ref[:, 2 * rank : 3 * rank] = dot(grads_ref[...], factor, lanes)
    stats_ref[:, 3 * rank : 4 * rank] = low_ref[...]


def direction_body(count, stats_ref, got_ref, hidden_ref, grads_ref, direction_ref, spread_ref, packed_ref):
    rank = spread_ref.shape[1]
    stats = stats_ref[...] + got_ref[...]
    length = jnp.sqrt(stats[:, :1] + EPSILON)
    along = stats[:, 1:2] / length
    direction = ((grads_ref[...].astype(F32) - along * (hidden_ref[...] / length)) / length).astype(BF16)
    direction_ref[...] = direction
    spread = (stats[:, 2 * rank : 3 * rank] - along * (stats[:, rank : 2 * rank] / length)) / length
    spread = spread.astype(BF16)
    spread_ref[...] = spread
    low = stats[:, 3 * rank : 4 * rank].astype(BF16)
    passes, columns = direction.shape
    packed_ref[:, :columns] = (ADAPTER_SCALE / count * dot(low, direction, ((0,), (0,)))).astype(BF16)
    packed_ref[:, columns:] = jnp.zeros_like(packed_ref[:, columns:])
    same = (iota((passes, passes), 0) == iota((passes, passes), 1)).astype(F32).astype(BF16)
    packed_ref[:, columns : columns + passes] = dot(spread, same, ((0,), (0,))).astype(BF16)


def first_sum_body(count, columns, sides, *refs):
    packed, pooled, out_ref = refs[:sides], refs[sides : 2 * sides], refs[-1]
    hidden = out_ref.shape[1] - columns
    passes = pooled[0].shape[0]
    first = sum(dot(a[:, columns : columns + passes], b[...]) for a, b in zip(packed, pooled))
    out_ref[:, :hidden] = (ADAPTER_SCALE / count * first).astype(BF16)
    out_ref[:, hidden:] = sum(a[:, :columns].astype(F32) for a in packed).astype(BF16)


def round_sum_body(own_ref, got_ref, *refs):
    refs[-1][...] = (own_ref[...].astype(F32) + got_ref[...].astype(F32)).astype(BF16)


def last_sum_body(own_ref, got_ref, *refs):
    first_ref, second_ref = refs[-2:]
    total = own_ref[...].astype(F32) + got_ref[...].astype(F32)
    hidden = first_ref.shape[1]
    first_ref[...] = total[:, :hidden]
    second_ref[...] = total[:, hidden:]


def activation_body(masks, first, member_ref, weight_ref, *refs):
    *before, out_ref, token_ref = refs
    pieces = [before.pop() for _ in masks][::-1]
    token_ref[...] = jnp.zeros_like(token_ref)
    columns = pieces[0].shape[1]

    def part(at, size):
        rows = pl.ds(at, size)
        if first:
            value = ADAPTER_SCALE * dot(before[0][...], before[1][:, rows])
        else:
            value = before[0][:, rows]
        for mask, piece in zip(masks, pieces):
            block = pl.ds(pl.multiple_of((member_ref[0] ^ mask) * columns, LANES), columns)
            value += dot(piece[...], weight_ref[rows, block], ((1,), (1,)))
        out_ref[:, rows] = value.astype(out_ref.dtype)

    total = out_ref.shape[1]

    @pl.loop(0, total // ROWS)
    def _(i):
        part(pl.multiple_of(i * ROWS, ROWS), ROWS)

    if total % ROWS:
        part(total - total % ROWS, total % ROWS)


def local(gradient_table, residual_input_rows, act, down_weight, adapter_input_factor, adapter_output_factor, lengths,
          owning_row_index):
    devices = lax.axis_size("dp")
    members = lax.axis_size("tensor")
    device = lax.axis_index("dp")
    member = lax.axis_index("tensor")
    passes = lengths.shape[1]
    owned, columns = gradient_table.shape
    rank, model = adapter_output_factor.shape
    hidden = act.shape[1]
    capacity = -(-passes // devices)
    slots = devices * capacity
    blocks = members // 2
    width = blocks * columns
    count = passes * devices
    dp_at = device.astype(jnp.int32).reshape(1)
    member_at = member.astype(jnp.int32).reshape(1)
    input_factor = adapter_input_factor.T

    def swap(x, axis, size, bit):
        return lax.ppermute(x, axis, [(i, i ^ bit) for i in range(size)])

    index = owning_row_index.reshape(1, -1)
    paired = devices & (devices - 1) == 0
    groups = devices // 2 if paired else 1
    *sent, last, my_index = call(
        functools.partial(route_body, passes, capacity, paired),
        [((slots // groups, columns), BF16)] * groups + [((passes, 1), jnp.int32)] * 2, "route",
        dp_at, near=(index, lengths, gradient_table),
    )
    if paired:
        came = [sent[0]] + [swap(sent[k], "dp", devices, 2 * k) for k in range(1, groups)]
    else:
        came = [lax.all_to_all(sent[0], "dp", 0, 0, tiled=True)]
    halves = (passes, blocks * columns)
    kept, away, pooled, low = call(
        project_body, [(halves, F32), (halves, F32), ((passes, hidden), BF16), ((passes, rank), F32)], "project",
        member_at, last, near=(input_factor, adapter_output_factor, residual_input_rows), far=(act, down_weight),
        scratch=[pltpu.VMEM(act.shape, BF16), pltpu.VMEM(down_weight.shape, BF16)]
        + [pltpu.SemaphoreType.DMA((len(cuts(hidden, ROWS)),))] * 2,
        flops=2 * passes * hidden * model,
    )
    if paired:
        half = ((slots // 2, columns), BF16)
        away, mine, other = call(
            functools.partial(meet_body, capacity), [(halves, BF16), half, half], "meet", away, *came
        )
        came = [mine, swap(other, "dp", devices, 1)]
    else:
        (away,) = call(round_body, [(halves, BF16)], "round", away)
    (grads,) = call(
        functools.partial(grads_body, owned, capacity), [((passes, columns), BF16)], "grads", dp_at, my_index, *came,
        flops=2 * WAIT,
    )
    away = swap(away, "tensor", members, 1)
    n = blocks // 2
    kept, out, pooled = call(
        functools.partial(sum_cores_body, columns),
        [((passes, n * columns), F32), ((passes, n * columns), BF16), (pooled.shape, BF16)],
        "sum_cores", member_at, kept, away, pooled,
    )
    far = [swap(pooled, "dp", devices, devices // 2)] if paired else []
    got = swap(out, "tensor", members, 2 * n)
    while n > 1:
        n //= 2
        kept, out = call(
            functools.partial(sum_chips_body, columns), [((passes, n * columns), F32), ((passes, n * columns), BF16)],
            "sum_chips", member_at, kept, got,
        )
        got = swap(out, "tensor", members, 2 * n)
    hidden_rows, stats = call(
        stats_body, [((passes, columns), F32), ((passes, LANES), F32)], "stats",
        member_at, kept, got, grads, low, adapter_output_factor,
    )
    bit = 1
    while 2 * bit < members:
        stats = stats + swap(stats, "tensor", members, bit)
        bit *= 2
    got = swap(stats, "tensor", members, bit)
    direction, spread, packed = call(
        functools.partial(direction_body, count),
        [((passes, columns), BF16), ((passes, rank), BF16), ((rank, columns + LANES * -(-passes // LANES)), BF16)],
        "direction", stats, got, hidden_rows, grads, flops=passes * columns * 64,
    )
    directions = {0: direction}
    bit = 2
    while bit < members:
        directions.update({k ^ bit: swap(v, "tensor", members, bit) for k, v in list(directions.items())})
        bit *= 2
    directions.update({k ^ 1: swap(v, "tensor", members, 1) for k, v in list(directions.items())})
    weight = pltpu.with_memory_space_constraint(down_weight, pltpu.VMEM)
    order = list(range(members))
    todo = [order[:1], order[1:-1], order[-1:]]
    token, activation = [], []

    def activate():
        masks = todo.pop(0)
        out, done = call(
            functools.partial(activation_body, masks, not activation),
            [((passes, hidden), F32 if todo else BF16), ((8, LANES), F32)], "activation",
            member_at, weight, *(activation or (spread, input_factor)), *[directions[k] for k in masks],
            flops=2 * passes * hidden * columns * len(masks),
        )
        activation[:] = [out]
        token[:] = [done]

    shapes = [((rank, hidden), F32), ((rank, columns), F32)]
    both = [((rank, hidden + columns), BF16)]
    first = functools.partial(first_sum_body, count, columns)
    if paired:
        got = swap(packed, "dp", devices, devices // 2)
        activate()
        (packed,) = call(functools.partial(first, 2), both, "sum_far", packed, got, pooled, *far, *token, keep=(weight,))
        bit = 1
        while bit < devices // 2:
            got = swap(packed, "dp", devices, bit)
            bit *= 2
            if todo:
                activate()
            if bit < devices // 2:
                (packed,) = call(round_sum_body, both, "sum_pairs", packed, got, *token, keep=(weight,))
            else:
                sums = call(last_sum_body, shapes, "sum_last", packed, got, *token)
    else:
        (packed,) = call(functools.partial(first, 1), both, "sum_own", packed, pooled)
        packed = lax.psum(packed.astype(F32), "dp")
        sums = packed[:, :hidden], packed[:, hidden:]
    while todo:
        activate()
    return activation[0], sums[0].T, sums[1]


def solution(mesh):
    placed = (
        P("dp", "tensor"),
        P("dp", "tensor"),
        P("dp", "tensor"),
        P("tensor", None),
        P("tensor", None),
        P(),
        P("dp", None),
        P(),
    )
    return jax.shard_map(
        local,
        mesh=mesh,
        in_specs=placed,
        out_specs=(P("dp", "tensor"), P("tensor", None), P(None, "tensor")),
        check_vma=False,
    )
```

```python
import functools

import jax
import jax.numpy as jnp
from jax import lax
from jax.experimental import pallas as pl
from jax.experimental.pallas import tpu as pltpu
from jax.sharding import PartitionSpec as P

ADAPTER_SCALE = 2.0
EPSILON = 1e-06
F32, BF16 = jnp.float32, jnp.bfloat16
LANES = 128
ROWS = 256
WIDE = 896
STEP = 512
WAIT = 5_000_000_000
VMEM = pl.BlockSpec(memory_space=pltpu.VMEM)
SMEM = pl.BlockSpec(memory_space=pltpu.SMEM)


def dot(a, b, dims=((1,), (0,))):
    return lax.dot_general(a, b, (dims, ((), ())), preferred_element_type=F32)


def call(body, outs, name, *args, near=(), far=(), keep=(), scratch=(), flops=0, limit=24):
    size = sum(a.size * a.dtype.itemsize for a in args + near + far)
    specs = [SMEM if a.dtype == jnp.int32 and a.size == 1 else VMEM for a in args]
    specs += [pl.BlockSpec(memory_space=pltpu.HBM)] * (len(near) + len(far)) + [VMEM] * len(keep)
    held = [pltpu.VMEM(a.shape, a.dtype) for a in near]
    held += [pltpu.SemaphoreType.DMA((len(near),))] if near else []

    def run(*refs):
        refs = list(refs)
        inputs = [refs.pop(0) for _ in args]
        distant = [refs.pop(0) for _ in near]
        inputs += [refs.pop(0) for _ in far]
        del refs[: len(keep)]
        if near:
            sems = refs.pop()
            here = refs[len(refs) - len(near) :]
            del refs[len(refs) - len(near) :]
            copies = [pltpu.make_async_copy(a, b, sems.at[i]) for i, (a, b) in enumerate(zip(distant, here))]
            for copy in copies:
                copy.start()
            inputs = (inputs, here, copies)
            body(inputs, *refs)
        else:
            body(*inputs, *refs)

    return pl.pallas_call(
        run,
        out_shape=[jax.ShapeDtypeStruct(*s) if isinstance(s, tuple) else s for s in outs],
        in_specs=specs,
        out_specs=[VMEM] * len(outs),
        scratch_shapes=list(scratch) + held,
        compiler_params=pltpu.CompilerParams(vmem_limit_bytes=limit << 20),
        cost_estimate=pl.CostEstimate(flops=flops, bytes_accessed=size, transcendentals=0),
        name=name,
    )(*args, *[pltpu.with_memory_space_constraint(a, pltpu.HBM) for a in near + far], *keep)


def cuts(total, step):
    return [(at, min(step, total - at)) for at in range(0, total, step)]


def iota(shape, dim):
    return lax.broadcasted_iota(jnp.int32, shape, dim)


def turned(column):
    n = column.shape[0]
    return jnp.sum(jnp.where(iota((n, n), 0) == iota((n, n), 1), column, 0), axis=0, keepdims=True)


def apart(device, other):
    return device % 2 ^ other % 2, (device // 2) ^ (other // 2)


def route_body(passes, capacity, paired, inputs, *refs):
    (device_ref,), (index_ref, lengths_ref, table_ref), copies = inputs
    *out_refs, last_ref, mine_ref = refs
    rows, slots = table_ref.shape[0], sum(ref.shape[0] for ref in out_refs)
    device = device_ref[0]
    copies[0].wait()
    index = index_ref[...]
    total = index.shape[1]
    mine = device * rows + iota((rows, total), 0)
    packed = iota((rows, total), 1) // passes
    dest = jnp.sum(jnp.where(index == mine, packed, 0), axis=1, keepdims=True)
    earlier = (dest == turned(dest)) & (iota((rows, rows), 1) < iota((rows, rows), 0))
    rank = jnp.sum(earlier.astype(jnp.int32), axis=1, keepdims=True)
    place = dest
    if paired:
        low, high = apart(dest, device)
        place = 2 * high + low
    slot = turned(place * capacity + rank)
    picker = (iota((slots, rows), 0) == slot).astype(F32).astype(BF16)
    own = iota((passes, total), 1) == device * passes + iota((passes, total), 0)
    mine_ref[...] = jnp.sum(jnp.where(own, index, 0), axis=1, keepdims=True)
    copies[1].wait()
    upto = jnp.where(iota((passes, passes), 1) <= iota((passes, passes), 0), lengths_ref[...], 0)
    last_ref[...] = jnp.sum(upto, axis=1, keepdims=True) - 1
    copies[2].wait()
    value = dot(picker, table_ref[...]).astype(BF16)
    size = slots // len(out_refs)
    for i, ref in enumerate(out_refs):
        ref[...] = value[i * size : (i + 1) * size]


def meet_body(capacity, away_ref, *refs):
    *blocks, out_ref, keep_ref, send_ref = refs
    out_ref[...] = away_ref[...].astype(BF16)
    rows = jnp.concatenate([ref[...] for ref in blocks], axis=0)
    n, total = keep_ref.shape[0], rows.shape[0]
    to, at = iota((n, total), 0), iota((n, total), 1)
    for low, ref in ((0, keep_ref), (1, send_ref)):
        picker = (at == (2 * (to // capacity) + low) * capacity + to % capacity).astype(F32).astype(BF16)
        ref[...] = dot(picker, rows).astype(BF16)


def project_body(inputs, kept_ref, away_ref, pooled_ref, low_ref, act_held, weight_held, act_sems, sems):
    (member_ref, last_ref, act_ref, weight_ref), (input_factor_ref, factor_ref, residual_ref), copies = inputs
    member = member_ref[0]
    columns = residual_ref.shape[1]
    hidden = act_ref.shape[1]
    pieces = []
    for i, (at, size) in enumerate(cuts(hidden, ROWS)):
        piece = slice(at, at + size)
        act_copy = pltpu.make_async_copy(act_ref.at[:, piece], act_held.at[:, piece], act_sems.at[i])
        act_copy.start()
        copy = pltpu.make_async_copy(weight_ref.at[piece], weight_held.at[piece], sems.at[i])
        copy.start()
        pieces.append((piece, act_copy, copy))
    picker = (last_ref[...] == iota((last_ref.shape[0], act_ref.shape[0]), 1)).astype(F32).astype(BF16)

    def places():
        for ref, core in ((away_ref, 1 - member % 2), (kept_ref, member % 2)):
            for j in range(ref.shape[1] // columns):
                start = pl.multiple_of((2 * j + core) * columns, LANES)
                yield ref, slice(j * columns, (j + 1) * columns), pl.ds(start, columns)

    for piece, act_copy, copy in pieces:
        act_copy.wait()
        pooled = dot(picker, act_held[:, piece]).astype(BF16)
        pooled_ref[:, piece] = pooled
        copy.wait()
        for ref, to, at in places():
            value = dot(pooled, weight_held[piece, at])
            if piece.start == 0:
                ref[:, to] = value
            else:
                ref[:, to] += value
    for copy in copies:
        copy.wait()
    low = dot(pooled_ref[...], input_factor_ref[...], ((1,), (1,)))
    low_ref[...] = low
    for ref, to, at in places():
        ref[:, to] += ADAPTER_SCALE * dot(low.astype(BF16), factor_ref[:, at])
    own = pl.ds(pl.multiple_of(member // 2 * columns, LANES), columns)
    kept_ref[:, own] += residual_ref[...].astype(F32)


def round_body(away_ref, out_ref):
    out_ref[...] = away_ref[...].astype(BF16)


def grads_body(owned, capacity, device_ref, index_ref, *refs):
    *parts, grads_ref = refs
    column = index_ref[...]
    row = turned(column)
    owner = column // owned
    earlier = (owner == row // owned) & (row < column)
    rank = jnp.sum(earlier.astype(jnp.int32), axis=1, keepdims=True)
    slots = parts[0].shape[0]
    low = jnp.zeros_like(owner)
    place = owner
    if len(parts) == 2:
        low, place = apart(owner, device_ref[0])
    total = 0
    for i, part in enumerate(parts):
        picker = (low == i) & (place * capacity + rank == iota((column.shape[0], slots), 1))
        total += dot(picker.astype(F32).astype(BF16), part[...])
    grads_ref[...] = total.astype(BF16)


def sum_cores_body(columns, member_ref, kept_ref, away_ref, pooled_ref, keep_ref, send_ref, pooled_out_ref):
    pooled_out_ref[...] = pooled_ref[...]
    n = keep_ref.shape[1] // columns
    side = member_ref[0] // 2 // n % 2
    for ref, half in ((keep_ref, side), (send_ref, 1 - side)):
        at = pl.ds(pl.multiple_of(half * n * columns, LANES), n * columns)
        ref[...] = (kept_ref[:, at] + away_ref[:, at].astype(F32)).astype(ref.dtype)


def sum_chips_body(columns, member_ref, kept_ref, got_ref, keep_ref, send_ref):
    n = keep_ref.shape[1] // columns
    side = member_ref[0] // 2 // n % 2
    for ref, half in ((keep_ref, side), (send_ref, 1 - side)):
        at = pl.ds(pl.multiple_of(half * n * columns, LANES), n * columns)
        ref[...] = (kept_ref[:, at] + got_ref[:, at].astype(F32)).astype(ref.dtype)


def stats_body(member_ref, kept_ref, got_ref, grads_ref, low_ref, factor_ref, hidden_ref, stats_ref):
    rank = low_ref.shape[1]
    columns = grads_ref.shape[1]
    hidden = kept_ref[...] + got_ref[...].astype(F32)
    hidden_ref[...] = hidden
    factor = factor_ref[:, pl.ds(pl.multiple_of(member_ref[0] * columns, LANES), columns)]
    high = hidden.astype(BF16)
    rest = (hidden - high.astype(F32)).astype(BF16)
    lanes = ((1,), (1,))
    stats_ref[...] = jnp.zeros_like(stats_ref)
    stats_ref[:, :1] = jnp.sum(hidden * hidden, axis=1, keepdims=True)
    stats_ref[:, 1:2] = jnp.sum(hidden * grads_ref[...].astype(F32), axis=1, keepdims=True)
    stats_ref[:, rank : 2 * rank] = dot(high, factor, lanes) + dot(rest, factor, lanes)
    stats_ref[:, 2 * rank : 3 * rank] = dot(grads_ref[...], factor, lanes)
    stats_ref[:, 3 * rank : 4 * rank] = low_ref[...]


def direction_body(count, stats_ref, got_ref, hidden_ref, grads_ref, direction_ref, spread_ref, packed_ref):
    rank = spread_ref.shape[1]
    stats = stats_ref[...] + got_ref[...]
    length = jnp.sqrt(stats[:, :1] + EPSILON)
    along = stats[:, 1:2] / length
    direction = ((grads_ref[...].astype(F32) - along * (hidden_ref[...] / length)) / length).astype(BF16)
    direction_ref[...] = direction
    spread = (stats[:, 2 * rank : 3 * rank] - along * (stats[:, rank : 2 * rank] / length)) / length
    spread = spread.astype(BF16)
    spread_ref[...] = spread
    low = stats[:, 3 * rank : 4 * rank].astype(BF16)
    passes, columns = direction.shape
    packed_ref[:, :columns] = (ADAPTER_SCALE / count * dot(low, direction, ((0,), (0,)))).astype(BF16)
    packed_ref[:, columns:] = jnp.zeros_like(packed_ref[:, columns:])
    same = (iota((passes, passes), 0) == iota((passes, passes), 1)).astype(F32).astype(BF16)
    packed_ref[:, columns : columns + passes] = dot(spread, same, ((0,), (0,))).astype(BF16)


def first_sum_body(count, columns, sides, *refs):
    packed, pooled, out_ref = refs[:sides], refs[sides : 2 * sides], refs[-1]
    hidden = out_ref.shape[1] - columns
    passes = pooled[0].shape[0]
    first = sum(dot(a[:, columns : columns + passes], b[...]) for a, b in zip(packed, pooled))
    out_ref[:, :hidden] = (ADAPTER_SCALE / count * first).astype(BF16)
    out_ref[:, hidden:] = sum(a[:, :columns].astype(F32) for a in packed).astype(BF16)


def round_sum_body(own_ref, got_ref, *refs):
    refs[-1][...] = (own_ref[...].astype(F32) + got_ref[...].astype(F32)).astype(BF16)


def last_sum_body(own_ref, got_ref, *refs):
    first_ref, second_ref = refs[-2:]
    total = own_ref[...].astype(F32) + got_ref[...].astype(F32)
    hidden = first_ref.shape[1]
    first_ref[...] = total[:, :hidden]
    second_ref[...] = total[:, hidden:]


def activation_body(masks, first, member_ref, weight_ref, *refs):
    *before, out_ref, token_ref = refs
    pieces = [before.pop() for _ in masks][::-1]
    token_ref[...] = jnp.zeros_like(token_ref)
    columns = pieces[0].shape[1]

    def part(at, size):
        rows = pl.ds(at, size)
        if first:
            value = ADAPTER_SCALE * dot(before[0][...], before[1][:, rows])
        else:
            value = before[0][:, rows]
        for mask, piece in zip(masks, pieces):
            block = pl.ds(pl.multiple_of((member_ref[0] ^ mask) * columns, LANES), columns)
            value += dot(piece[...], weight_ref[rows, block], ((1,), (1,)))
        out_ref[:, rows] = value.astype(out_ref.dtype)

    total = out_ref.shape[1]

    @pl.loop(0, total // WIDE)
    def _(i):
        part(pl.multiple_of(i * WIDE, WIDE), WIDE)

    if total % WIDE:
        part(total - total % WIDE, total % WIDE)


def local(gradient_table, residual_input_rows, act, down_weight, adapter_input_factor, adapter_output_factor, lengths,
          owning_row_index):
    devices = lax.axis_size("dp")
    members = lax.axis_size("tensor")
    device = lax.axis_index("dp")
    member = lax.axis_index("tensor")
    passes = lengths.shape[1]
    owned, columns = gradient_table.shape
    rank, model = adapter_output_factor.shape
    hidden = act.shape[1]
    capacity = -(-passes // devices)
    slots = devices * capacity
    blocks = members // 2
    width = blocks * columns
    count = passes * devices
    dp_at = device.astype(jnp.int32).reshape(1)
    member_at = member.astype(jnp.int32).reshape(1)
    input_factor = adapter_input_factor.T

    def swap(x, axis, size, bit):
        return lax.ppermute(x, axis, [(i, i ^ bit) for i in range(size)])

    index = owning_row_index.reshape(1, -1)
    paired = devices & (devices - 1) == 0
    groups = devices // 2 if paired else 1
    *sent, last, my_index = call(
        functools.partial(route_body, passes, capacity, paired),
        [((slots // groups, columns), BF16)] * groups + [((passes, 1), jnp.int32)] * 2, "route",
        dp_at, near=(index, lengths, gradient_table),
    )
    if paired:
        came = [sent[0]] + [swap(sent[k], "dp", devices, 2 * k) for k in range(1, groups)]
    else:
        came = [lax.all_to_all(sent[0], "dp", 0, 0, tiled=True)]
    halves = (passes, blocks * columns)
    kept, away, pooled, low = call(
        project_body, [(halves, F32), (halves, F32), ((passes, hidden), BF16), ((passes, rank), F32)], "project",
        member_at, last, near=(input_factor, adapter_output_factor, residual_input_rows), far=(act, down_weight),
        scratch=[pltpu.VMEM(act.shape, BF16), pltpu.VMEM(down_weight.shape, BF16)]
        + [pltpu.SemaphoreType.DMA((len(cuts(hidden, ROWS)),))] * 2,
        flops=2 * passes * hidden * model,
    )
    if paired:
        half = ((slots // 2, columns), BF16)
        away, mine, other = call(
            functools.partial(meet_body, capacity), [(halves, BF16), half, half], "meet", away, *came
        )
        came = [mine, swap(other, "dp", devices, 1)]
    else:
        (away,) = call(round_body, [(halves, BF16)], "round", away)
    (grads,) = call(
        functools.partial(grads_body, owned, capacity), [((passes, columns), BF16)], "grads", dp_at, my_index, *came,
        flops=2 * WAIT,
    )
    away = swap(away, "tensor", members, 1)
    n = blocks // 2
    kept, out, pooled = call(
        functools.partial(sum_cores_body, columns),
        [((passes, n * columns), F32), ((passes, n * columns), BF16), (pooled.shape, BF16)],
        "sum_cores", member_at, kept, away, pooled,
    )
    far = [swap(pooled, "dp", devices, devices // 2)] if paired else []
    got = swap(out, "tensor", members, 2 * n)
    while n > 1:
        n //= 2
        kept, out = call(
            functools.partial(sum_chips_body, columns), [((passes, n * columns), F32), ((passes, n * columns), BF16)],
            "sum_chips", member_at, kept, got,
        )
        got = swap(out, "tensor", members, 2 * n)
    hidden_rows, stats = call(
        stats_body, [((passes, columns), F32), ((passes, LANES), F32)], "stats",
        member_at, kept, got, grads, low, adapter_output_factor,
    )
    bit = 1
    while 2 * bit < members:
        stats = stats + swap(stats, "tensor", members, bit)
        bit *= 2
    got = swap(stats, "tensor", members, bit)
    direction, spread, packed = call(
        functools.partial(direction_body, count),
        [((passes, columns), BF16), ((passes, rank), BF16), ((rank, columns + LANES * -(-passes // LANES)), BF16)],
        "direction", stats, got, hidden_rows, grads, flops=passes * columns * 64,
    )
    directions = {0: direction}
    bit = 2
    while bit < members:
        directions.update({k ^ bit: swap(v, "tensor", members, bit) for k, v in list(directions.items())})
        bit *= 2
    directions.update({k ^ 1: swap(v, "tensor", members, 1) for k, v in list(directions.items())})
    weight = pltpu.with_memory_space_constraint(down_weight, pltpu.VMEM)
    order = list(range(members))
    todo = [order[:1], order[1:-1], order[-1:]]
    token, activation = [], []

    def activate():
        masks = todo.pop(0)
        out, done = call(
            functools.partial(activation_body, masks, not activation),
            [((passes, hidden), F32 if todo else BF16), ((8, LANES), F32)], "activation",
            member_at, weight, *(activation or (spread, input_factor)), *[directions[k] for k in masks],
            flops=2 * passes * hidden * columns * len(masks),
        )
        activation[:] = [out]
        token[:] = [done]

    shapes = [((rank, hidden), F32), ((rank, columns), F32)]
    both = [((rank, hidden + columns), BF16)]
    first = functools.partial(first_sum_body, count, columns)
    if paired:
        got = swap(packed, "dp", devices, devices // 2)
        activate()
        (packed,) = call(functools.partial(first, 2), both, "sum_far", packed, got, pooled, *far, *token, keep=(weight,))
        bit = 1
        while bit < devices // 2:
            got = swap(packed, "dp", devices, bit)
            bit *= 2
            if todo:
                activate()
            if bit < devices // 2:
                (packed,) = call(round_sum_body, both, "sum_pairs", packed, got, *token, keep=(weight,))
            else:
                sums = call(last_sum_body, shapes, "sum_last", packed, got, *token)
    else:
        (packed,) = call(functools.partial(first, 1), both, "sum_own", packed, pooled)
        packed = lax.psum(packed.astype(F32), "dp")
        sums = packed[:, :hidden], packed[:, hidden:]
    while todo:
        activate()
    return activation[0], sums[0].T, sums[1]


def solution(mesh):
    placed = (
        P("dp", "tensor"),
        P("dp", "tensor"),
        P("dp", "tensor"),
        P("tensor", None),
        P("tensor", None),
        P(),
        P("dp", None),
        P(),
    )
    return jax.shard_map(
        local,
        mesh=mesh,
        in_specs=placed,
        out_specs=(P("dp", "tensor"), P("tensor", None), P(None, "tensor")),
        check_vma=False,
    )
```
